256 devices in a mesh: replica: 32 (over x, z_hi, core), tensor: 8 (over y, z_lo).
Axes of the slice: x: 4, y: 4, z: 8 (z_hi: 4, z_lo: 2; z = z_hi * 2 + z_lo), core: 2. Of those that a mesh axis runs over, the one named last changes fastest.
Arguments:
- queries: bfloat16 [16384, 4096], P('replica', 'tensor'), may hold values from -240 to 240
- keys: bfloat16 [16384, 1024], P('replica', 'tensor'), may hold values from -6 to 6
- values_in: bfloat16 [16384, 1024], P('replica', 'tensor'), may hold values from -36 to 36
- out_grad: bfloat16 [16384, 4096], P(('replica', 'tensor')), may hold values from -6 to 6
- proj_local: bfloat16 [32, 4096, 4096], P('replica', 'tensor'), may hold values from -0.1875 to 0.1875
- outer_weight: float32 [4096, 4096], P('tensor', 'replica'), may hold values from -0.09375 to 0.09375
- momentum: float32 [4096, 4096], P('tensor', 'replica'), may hold values from -0.06 to 0.06
Outputs:
- attn_out: bfloat16 [16384, 4096], P(('replica', 'tensor'))
- query_grad: bfloat16 [16384, 4096], P('replica', 'tensor')
- key_grad: bfloat16 [16384, 1024], P('replica', 'tensor')
- value_grad: bfloat16 [16384, 1024], P('replica', 'tensor')
- new_local: bfloat16 [32, 4096, 4096], P('replica', 'tensor')
- new_outer: float32 [4096, 4096], P('tensor', 'replica')
- new_momentum: float32 [4096, 4096], P('tensor', 'replica')
The draws below stay inside these ranges and needn't reach their ends.
All inputs are finite; a program needn't handle non-finite values.
Results may differ from the reference program's by a relative error of at most 0.017.
Values may be sent and summed in bfloat16 or wider, within the bound.
No kernel may reach another device: no remote copies, remote signals or barrier semaphores. Data moves between devices by JAX's collectives and lax.ppermute only.
A program may use at most 192 MiB of HBM per device.

```python
import jax
import jax.numpy as jnp
from jax import lax

D = 4096
HEADS = 32
KVH = 8
HD = 128
TOK = 512
ISLANDS = 32
TOKENS = 16384
HQ = 4096
KVW = 1024
N_TENSOR = 8


def shared_keys(key):
    return jnp.clip(jax.random.normal(jax.random.fold_in(key, 11), (TOKENS, KVW), jnp.float32), -6.0, 6.0)


def head_ramp(top):
    place = jnp.arange(KVW, dtype=jnp.float32) // HD
    return top ** (place / max(KVH - 1, 1))


def draw_keys(key, part):
    base = shared_keys(key)
    return base.astype(jnp.bfloat16)


def draw_queries(key, part):
    key = jax.random.fold_in(key, 5)
    return jnp.clip(jax.random.normal(key, (TOKENS, HQ), jnp.float32), -6.0, 6.0).astype(jnp.bfloat16)


def draw_values_in(key, part):
    key = jax.random.fold_in(key, 7)
    fresh = jnp.clip(jax.random.normal(key, (TOKENS, KVW), jnp.float32), -6.0, 6.0)
    return (fresh * head_ramp(3.0)[None, :]).astype(jnp.bfloat16)


def strengthened(result, key, source, target, blocks, factor):
    owner, partner = [(jnp.arange(result.shape[position]) // (result.shape[position] // blocks)).reshape([-1 if axis == position else 1 for axis in range(result.ndim)]) for position in (source, target)]
    chosen = jax.random.permutation(key, blocks)[partner]
    strong = (owner == chosen) | (owner == (partner + blocks // 2) % blocks)
    return jnp.where(strong, factor * result, result)


def shard_levels(own_key, shape, split, smallest, top_value):
    level, own = 1.0, jax.random.fold_in(own_key, 6)
    for axis_at, shards_of in split:
        draws = jnp.exp(jax.random.uniform(jax.random.fold_in(own, axis_at), (shards_of,), jnp.float32, smallest / len(split), top_value / len(split)))
        level = level * jnp.repeat(draws, shape[axis_at] // shards_of).reshape([-1 if axis == axis_at else 1 for axis in range(len(shape))])
    return level


def scatter_about(own_key, shape, spread, most, split=(), held_as=jnp.bfloat16):
    entries = spread * jax.random.normal(own_key, shape, jnp.float32)
    if split:
        entries = entries * shard_levels(own_key, shape, split, -0.22, 0.18)
    return jnp.clip(entries, -most, most).astype(held_as)


def heavy_noise(rng, extent, spread, reach, split, heavy, held_as=jnp.bfloat16):
    entries = spread * jax.random.normal(rng, extent, jnp.float32)
    if split:
        entries = entries * shard_levels(rng, extent, split, -0.22, 0.18)
    return jnp.clip(strengthened(entries, jax.random.fold_in(rng, 3), *heavy), -reach, reach).astype(held_as)


def setup_inputs(seed: int = 0) -> dict:
    key_list = jax.random.split(jax.random.key(seed), 8)
    queries = draw_queries(jax.random.fold_in(key_list[7], 71), 0)
    keys = draw_keys(jax.random.fold_in(key_list[7], 71), 0)
    values_in = draw_values_in(jax.random.fold_in(key_list[7], 71), 0)
    out_grad = scatter_about(key_list[3], (TOKENS, D), 1.0, 6.0, ((0, 256),))
    proj_local = heavy_noise(key_list[4], (ISLANDS, HQ, D), HQ ** -0.5, 0.1875, ((0, 32), (1, 8)), (0, 2, 32, 2.75))
    outer_weight = scatter_about(key_list[5], (HQ, D), HQ ** -0.5, 0.09375, ((0, 8), (1, 32)), jnp.float32)
    momentum = scatter_about(key_list[6], (HQ, D), 0.01, 0.06, ((0, 8), (1, 32)), jnp.float32)
    return {"queries": queries, "keys": keys, "values_in": values_in, "out_grad": out_grad, "proj_local": proj_local, "outer_weight": outer_weight, "momentum": momentum}


step_size = 0.02
mu_outer = 0.9
lr_outer = 0.7
mix_share = 0.5
eps_norm = 1e-06

def island_pass(queries, keys, values_in, out_grad, weight):
    group_size = HEADS // KVH
    scale_factor = HD ** (-0.5)
    length = queries.shape[0]
    query_grid = queries.reshape(length, KVH, group_size, HD).astype(jnp.float32)
    key_grid = keys.reshape(length, KVH, HD).astype(jnp.float32)
    value_grid = values_in.reshape(length, KVH, HD).astype(jnp.float32)
    scores = jnp.einsum('tkgd,ukd->kgtu', query_grid, key_grid) * scale_factor
    causal = jnp.arange(length)[:, None] >= jnp.arange(length)[None, :]
    scores = jnp.where(causal, scores, -jnp.inf)
    highest = lax.optimization_barrier(jnp.max(scores, axis=-1, keepdims=True))
    expon = jnp.exp(scores - highest)
    probs = expon / lax.optimization_barrier(jnp.sum(expon, axis=-1, keepdims=True))
    probs_half = probs.astype(jnp.bfloat16)
    context = jnp.einsum('kgtu,ukd->tkgd', probs_half.astype(jnp.float32), value_grid)
    context = context.astype(jnp.bfloat16).reshape(length, HQ)
    width = HQ // N_TENSOR
    parts = jnp.einsum('tnw,nwd->ntd', context.reshape(length, N_TENSOR, width).astype(jnp.float32), weight.reshape(N_TENSOR, width, D).astype(jnp.float32))
    parts = lax.optimization_barrier(parts.astype(jnp.bfloat16)).astype(jnp.float32)
    attn_out = lax.optimization_barrier(jnp.sum(parts, axis=0)).astype(jnp.bfloat16)
    ctx_grad = jnp.dot(out_grad, weight.T, preferred_element_type=jnp.float32).astype(jnp.bfloat16)
    grad_proj = jnp.dot(context.T, out_grad, preferred_element_type=jnp.float32)
    grad_grid = ctx_grad.reshape(length, KVH, group_size, HD).astype(jnp.float32)
    prob_grad = jnp.einsum('tkgd,ukd->kgtu', grad_grid, value_grid)
    inner = lax.optimization_barrier(jnp.sum(prob_grad * probs, axis=-1, keepdims=True))
    score_grad = (probs * (prob_grad - inner) * scale_factor).astype(jnp.bfloat16).astype(jnp.float32)
    query_grad = jnp.einsum('kgtu,ukd->tkgd', score_grad, key_grid).astype(jnp.bfloat16).reshape(length, HQ)
    key_grad = jnp.einsum('kgtu,tkgd->ukd', score_grad, query_grid).astype(jnp.bfloat16).reshape(length, KVW)
    value_grad = jnp.einsum('kgtu,tkgd->ukd', probs_half.astype(jnp.float32), grad_grid).astype(jnp.bfloat16).reshape(length, KVW)
    grad_rms = jnp.sqrt(jnp.sum(grad_proj * grad_proj) / (HQ * D) + eps_norm)
    stepped = (weight.astype(jnp.float32) - step_size * grad_proj / grad_rms).astype(jnp.bfloat16)
    return (attn_out, query_grad, key_grad, value_grad, stepped)

def reference(queries, keys, values_in, out_grad, proj_local, outer_weight, momentum):

    def one_island(island):
        start = (island * TOK).astype(jnp.int32)
        return island_pass(lax.dynamic_slice_in_dim(queries, start, TOK, 0), lax.dynamic_slice_in_dim(keys, start, TOK, 0), lax.dynamic_slice_in_dim(values_in, start, TOK, 0), lax.dynamic_slice_in_dim(out_grad, start, TOK, 0), lax.dynamic_index_in_dim(proj_local, island.astype(jnp.int32), 0, keepdims=False))
    attn_out, query_grad, key_grad, value_grad, stepped = lax.map(one_island, jnp.arange(ISLANDS, dtype=jnp.int32))
    total = lax.optimization_barrier(jnp.sum(proj_local.astype(jnp.float32), axis=0))
    delta = outer_weight - total / ISLANDS
    new_momentum = mu_outer * momentum + delta
    new_outer = outer_weight - lr_outer * (mu_outer * new_momentum + delta)
    outer_half = new_outer.astype(jnp.bfloat16).astype(jnp.float32)
    new_local = (mix_share * stepped.astype(jnp.float32) + (1.0 - mix_share) * outer_half[None]).astype(jnp.bfloat16)
    return (attn_out.reshape(TOKENS, D), query_grad.reshape(TOKENS, HQ), key_grad.reshape(TOKENS, KVW), value_grad.reshape(TOKENS, KVW), new_local, new_outer, new_momentum)
```

```python
import jax
import jax.numpy as jnp
from jax import lax
from jax.experimental import pallas as pl
from jax.experimental.pallas import tpu as pltpu
from jax.sharding import PartitionSpec as P

D = 4096
HEADS = 32
KVH = 8
HD = 128
TOK = 512
ISLANDS = 32
GROUP = HEADS // KVH
NX = 4
NZ = 4
NY = 4
NL = 2
SHARE = 128
ROWS = 64

step_size = 0.02
mu_outer = 0.9
lr_outer = 0.7
mix_share = 0.5
eps_norm = 1e-06
scale_factor = HD ** (-0.5)

BF = jnp.bfloat16
F32 = jnp.float32
VMEM_LIMIT = 48 * 1024 * 1024


def params():
    return pltpu.CompilerParams(vmem_limit_bytes=VMEM_LIMIT)


def cost(flops, nbytes, trans=0):
    return pl.CostEstimate(flops=int(flops), bytes_accessed=int(nbytes), transcendentals=int(trans))


def replica_shift(v, dx, dz, dc):
    def at(x, z, c):
        return (x * NZ + z) * 2 + c

    pairs = [
        (at(x, z, c), at((x + dx) % NX, (z + dz) % NZ, (c + dc) % 2))
        for x in range(NX)
        for z in range(NZ)
        for c in range(2)
    ]
    return lax.ppermute(v, "replica", pairs)


def tensor_shift(v, dy, dl):
    pairs = [
        (y * NL + l, ((y + dy) % NY) * NL + (l + dl) % NL) for y in range(NY) for l in range(NL)
    ]
    return lax.ppermute(v, "tensor", pairs)


def share_column(pos, dx, dz, dc):
    x, z, c = pos[0], pos[1], pos[2]
    return (((x + dx) % NX) * NZ + (z + dz) % NZ) * 2 + (c + dc) % 2


def token_block(pos, dy, dl):
    return ((pos[3] + dy) % NY) * NL + (pos[4] + dl) % NL


def split_kernel(pos, w_ref, *outs):
    for k in range(NX):
        for j in range(NZ):
            col = pl.multiple_of(share_column(pos, k, j, 1) * SHARE, SHARE)
            outs[k][:, j * SHARE : (j + 1) * SHARE] = w_ref[:, pl.ds(col, SHARE)]


def split(pos, weight):
    rows = 128
    piece = jax.ShapeDtypeStruct((TOK, NZ * SHARE), BF)
    return pl.pallas_call(
        split_kernel,
        out_shape=[piece] * NX,
        grid_spec=pltpu.PrefetchScalarGridSpec(
            num_scalar_prefetch=1,
            grid=(TOK // rows,),
            in_specs=[pl.BlockSpec((rows, D), lambda i, pos: (i, 0))],
            out_specs=[pl.BlockSpec((rows, NZ * SHARE), lambda i, pos: (i, 0))] * NX,
        ),
        compiler_params=params(),
        cost_estimate=cost(0, 4 << 20),
        name="split",
    )(pos, weight)


def core_add_kernel(pos, w_ref, r_ref, o_ref):
    o_ref[...] = (w_ref[...].astype(F32) + r_ref[...].astype(F32)).astype(BF)


def core_add(pos, weight, got, k):
    return pl.pallas_call(
        core_add_kernel,
        out_shape=jax.ShapeDtypeStruct((TOK, NZ * SHARE), BF),
        grid_spec=pltpu.PrefetchScalarGridSpec(
            num_scalar_prefetch=1,
            grid=(NZ,),
            in_specs=[
                pl.BlockSpec((TOK, SHARE), lambda j, pos: (0, share_column(pos, k, j, 0))),
                pl.BlockSpec((TOK, SHARE), lambda j, pos: (0, j)),
            ],
            out_specs=pl.BlockSpec((TOK, SHARE), lambda j, pos: (0, j)),
        ),
        compiler_params=params(),
        cost_estimate=cost(0, 3 << 19),
        name="core_add",
    )(pos, weight, got)


def x_add_kernel(pos, w_ref, r_ref, a_ref, b_ref, c_ref, *outs):
    for j in range(NZ):
        at = slice(j * SHARE, (j + 1) * SHARE)
        col = pl.multiple_of(share_column(pos, 0, j, 0) * SHARE, SHARE)
        total = w_ref[:, pl.ds(col, SHARE)].astype(F32) + r_ref[:, at].astype(F32)
        total = total + a_ref[:, at].astype(F32)
        total = total + b_ref[:, at].astype(F32)
        total = total + c_ref[:, at].astype(F32)
        outs[j][...] = total.astype(BF)


def x_add(pos, weight, got, parts):
    rows = 128
    wide = pl.BlockSpec((rows, NZ * SHARE), lambda i, pos: (i, 0))
    return pl.pallas_call(
        x_add_kernel,
        out_shape=[jax.ShapeDtypeStruct((TOK, SHARE), BF)] * NZ,
        grid_spec=pltpu.PrefetchScalarGridSpec(
            num_scalar_prefetch=1,
            grid=(TOK // rows,),
            in_specs=[pl.BlockSpec((rows, D), lambda i, pos: (i, 0))] + [wide] * 4,
            out_specs=[pl.BlockSpec((rows, SHARE), lambda i, pos: (i, 0))] * NZ,
        ),
        compiler_params=params(),
        cost_estimate=cost(0, 3 << 20),
        name="x_add",
    )(pos, weight, got, *parts)


def outer_kernel(s_ref, a_ref, b_ref, c_ref, ow_ref, mo_ref, no_ref, nm_ref, nb_ref):
    total = s_ref[...].astype(F32) + a_ref[...].astype(F32)
    total = total + b_ref[...].astype(F32)
    total = total + c_ref[...].astype(F32)
    outer = ow_ref[...]
    delta = outer - total / ISLANDS
    moment = mu_outer * mo_ref[...] + delta
    new = outer - lr_outer * (mu_outer * moment + delta)
    no_ref[...] = new
    nm_ref[...] = moment
    nb_ref[...] = new.astype(BF)


def outer_update(own, parts, outer_weight, momentum):
    f32 = jax.ShapeDtypeStruct((TOK, SHARE), F32)
    return pl.pallas_call(
        outer_kernel,
        out_shape=[f32, f32, jax.ShapeDtypeStruct((TOK, SHARE), BF)],
        compiler_params=params(),
        cost_estimate=cost(0, 2 << 20),
        name="outer_update",
    )(own, *parts, outer_weight, momentum)


def causal_mask(rows, cols, first):
    return lax.broadcasted_iota(jnp.int32, (rows, cols), 0) + first >= lax.broadcasted_iota(
        jnp.int32, (rows, cols), 1
    )


def dot(a, b, ca, cb):
    return lax.dot_general(a, b, (((ca,), (cb,)), ((), ())), preferred_element_type=F32)


def probs_of(q, k, first, rows, cols):
    scores = dot(q, k, 1, 1) * scale_factor
    scores = jnp.where(causal_mask(rows, cols, first), scores, -jnp.inf)
    highest = jnp.max(scores, axis=-1, keepdims=True)
    expon = jnp.exp(scores - highest)
    return expon / jnp.sum(expon, axis=-1, keepdims=True)


HALF = TOK // 2


def forward_kernel(q_ref, k_ref, v_ref, o_ref):
    for part in range(2):
        first, cols = part * HALF, (part + 1) * HALF
        q = q_ref[first : first + HALF, :]
        probs = probs_of(q, k_ref[0:cols, :], first, HALF, cols)
        o_ref[first : first + HALF, :] = dot(probs.astype(BF), v_ref[0:cols, :], 1, 0).astype(BF)


def forward(queries, keys, values):
    head = pl.BlockSpec((TOK, HD), lambda h: (0, h))
    kv = pl.BlockSpec((TOK, HD), lambda h: (0, 0))
    return pl.pallas_call(
        forward_kernel,
        out_shape=jax.ShapeDtypeStruct((TOK, GROUP * HD), BF),
        grid=(GROUP,),
        in_specs=[head, kv, kv],
        out_specs=head,
        compiler_params=params(),
        cost_estimate=cost(5e8, 2 << 20, 1 << 20),
        name="forward",
    )(queries, keys, values)


def backward_kernel(q_ref, k_ref, v_ref, g_ref, dq_ref, dk_ref, dv_ref, dk_acc, dv_acc):
    h = pl.program_id(0)

    @pl.when(h == 0)
    def _():
        dk_acc[...] = jnp.zeros_like(dk_acc)
        dv_acc[...] = jnp.zeros_like(dv_acc)

    for part in range(2):
        first, cols = part * HALF, (part + 1) * HALF
        rows = slice(first, first + HALF)
        q, g = q_ref[rows, :], g_ref[rows, :]
        k, v = k_ref[0:cols, :], v_ref[0:cols, :]
        probs = probs_of(q, k, first, HALF, cols)
        prob_grad = dot(g, v, 1, 1)
        inner = jnp.sum(prob_grad * probs, axis=-1, keepdims=True)
        score_grad = (probs * (prob_grad - inner) * scale_factor).astype(BF)
        dq_ref[rows, :] = dot(score_grad, k, 1, 0).astype(BF)
        dk_acc[0:cols, :] += dot(score_grad, q, 0, 0)
        dv_acc[0:cols, :] += dot(probs.astype(BF), g, 0, 0)

    @pl.when(h == GROUP - 1)
    def _():
        dk_ref[...] = dk_acc[...].astype(BF)
        dv_ref[...] = dv_acc[...].astype(BF)


def backward(queries, keys, values, ctx_grad):
    head = pl.BlockSpec((TOK, HD), lambda h: (0, h))
    kv = pl.BlockSpec((TOK, HD), lambda h: (0, 0))
    small = jax.ShapeDtypeStruct((TOK, HD), BF)
    return pl.pallas_call(
        backward_kernel,
        out_shape=[jax.ShapeDtypeStruct((TOK, GROUP * HD), BF), small, small],
        grid=(GROUP,),
        in_specs=[head, kv, kv, head],
        out_specs=[head, kv, kv],
        scratch_shapes=[pltpu.VMEM((TOK, HD), F32), pltpu.VMEM((TOK, HD), F32)],
        compiler_params=params(),
        cost_estimate=cost(1.3e9, 3 << 20, 1 << 20),
        name="backward",
    )(queries, keys, values, ctx_grad)


SHIFTS = [(dy, dl) for dy in range(NY) for dl in range(NL)]
TILE = 512


def term_kernel(pos, c_ref, w_ref, *rest):
    outs, held = rest[:-1], rest[-1]
    held[...] = dot(c_ref[...], w_ref[...], 1, 0).astype(BF)
    for (dy, dl), out in zip(SHIFTS, outs):
        row = pl.multiple_of(token_block(pos, dy, dl) * ROWS, ROWS)
        out[...] = held[pl.ds(row, ROWS), :]


def term(pos, context, weight):
    return pl.pallas_call(
        term_kernel,
        out_shape=[jax.ShapeDtypeStruct((ROWS, D), BF)] * len(SHIFTS),
        grid_spec=pltpu.PrefetchScalarGridSpec(
            num_scalar_prefetch=1,
            grid=(D // TILE,),
            in_specs=[
                pl.BlockSpec((TOK, GROUP * HD), lambda i, pos: (0, 0)),
                pl.BlockSpec((GROUP * HD, TILE), lambda i, pos: (0, i)),
            ],
            out_specs=[pl.BlockSpec((ROWS, TILE), lambda i, pos: (0, i))] * len(SHIFTS),
            scratch_shapes=[pltpu.VMEM((TOK, TILE), BF)],
        ),
        compiler_params=params(),
        cost_estimate=cost(2.1e9, 9 << 20),
        name="term",
    )(pos, context, weight)


def attn_sum_kernel(*refs):
    total = refs[0][...].astype(F32)
    for ref in refs[1:-1]:
        total = total + ref[...].astype(F32)
    refs[-1][...] = total.astype(BF)


def attn_sum(parts):
    spec = pl.BlockSpec((ROWS, 1024), lambda i: (0, i))
    return pl.pallas_call(
        attn_sum_kernel,
        out_shape=jax.ShapeDtypeStruct((ROWS, D), BF),
        grid=(D // 1024,),
        in_specs=[spec] * len(parts),
        out_specs=spec,
        compiler_params=params(),
        cost_estimate=cost(0, 9 << 19),
        name="attn_sum",
    )(*parts)


def grads_kernel(pos, *refs):
    pieces, (w_ref, c_ref, proj_ref, ctx_ref, sq_ref, held, turned, acc, sq) = (
        refs[: len(SHIFTS)],
        refs[len(SHIFTS) :],
    )
    i = pl.program_id(0)

    @pl.when(i == 0)
    def _():
        turned[...] = c_ref[...].T
        acc[...] = jnp.zeros_like(acc)
        sq[...] = jnp.zeros_like(sq)

    for (dy, dl), piece in zip(SHIFTS, pieces):
        row = pl.multiple_of(token_block(pos, -dy, -dl) * ROWS, ROWS)
        held[pl.ds(row, ROWS), :] = piece[...]
    grad = held[...]
    acc[...] += dot(grad, w_ref[...], 1, 1)
    proj = dot(turned[...], grad, 1, 0)
    proj_ref[...] = proj.astype(BF)
    sq[...] += jnp.sum((proj * proj).reshape(TOK // 8, 8, TILE), axis=0)

    @pl.when(i == pl.num_programs(0) - 1)
    def _():
        ctx_ref[...] = acc[...].astype(BF)
        sq_ref[...] = jnp.broadcast_to(jnp.sum(sq[...], axis=(0, 1), keepdims=True), (8, 128))


def grads(pos, pieces, weight, context):
    hq = GROUP * HD
    return pl.pallas_call(
        grads_kernel,
        out_shape=[
            jax.ShapeDtypeStruct((hq, D), BF),
            jax.ShapeDtypeStruct((TOK, hq), BF),
            jax.ShapeDtypeStruct((8, 128), F32),
        ],
        grid_spec=pltpu.PrefetchScalarGridSpec(
            num_scalar_prefetch=1,
            grid=(D // TILE,),
            in_specs=[pl.BlockSpec((ROWS, TILE), lambda i, pos: (0, i))] * len(SHIFTS)
            + [
                pl.BlockSpec((hq, TILE), lambda i, pos: (0, i)),
                pl.BlockSpec((TOK, hq), lambda i, pos: (0, 0)),
            ],
            out_specs=[
                pl.BlockSpec((hq, TILE), lambda i, pos: (0, i)),
                pl.BlockSpec((TOK, hq), lambda i, pos: (0, 0)),
                pl.BlockSpec((8, 128), lambda i, pos: (0, 0)),
            ],
            scratch_shapes=[
                pltpu.VMEM((TOK, TILE), BF),
                pltpu.VMEM((hq, TOK), BF),
                pltpu.VMEM((TOK, hq), F32),
                pltpu.VMEM((8, TILE), F32),
            ],
        ),
        compiler_params=params(),
        cost_estimate=cost(4.3e9, 13 << 20),
        name="grads",
    )(pos, *pieces, weight, context)


def stepped_kernel(sq_ref, w_ref, g_ref, o_ref):
    rate = step_size / jnp.sqrt(sq_ref[0:1, 0:1] / (HEADS * HD * D) + eps_norm)
    o_ref[...] = (w_ref[...].astype(F32) - rate * g_ref[...].astype(F32)).astype(BF)


def stepped_of(square, weight, proj_grad):
    spec = pl.BlockSpec((128, D), lambda i: (i, 0))
    return pl.pallas_call(
        stepped_kernel,
        out_shape=jax.ShapeDtypeStruct((TOK, D), BF),
        grid=(TOK // 128,),
        in_specs=[pl.BlockSpec((8, 128), lambda i: (0, 0)), spec, spec],
        out_specs=spec,
        compiler_params=params(),
        cost_estimate=cost(0, 12 << 20),
        name="stepped",
    )(square, weight, proj_grad)


def mix_kernel(pos, s_ref, *refs):
    o_ref = refs[-1]
    n = 0
    for c in range(2):
        for k in range(NX):
            piece = refs[n]
            n += 1
            for j in range(NZ):
                at = pl.ds(pl.multiple_of(share_column(pos, -k, -j, c) * SHARE, SHARE), SHARE)
                outer = piece[:, j * SHARE : (j + 1) * SHARE].astype(F32)
                local = s_ref[:, at].astype(F32)
                o_ref[:, at] = (mix_share * local + (1.0 - mix_share) * outer).astype(BF)


def mix(pos, stepped, pieces):
    rows = 128
    whole = pl.BlockSpec((rows, D), lambda i, pos: (i, 0))
    wide = pl.BlockSpec((rows, NZ * SHARE), lambda i, pos: (i, 0))
    return pl.pallas_call(
        mix_kernel,
        out_shape=jax.ShapeDtypeStruct((TOK, D), BF),
        grid_spec=pltpu.PrefetchScalarGridSpec(
            num_scalar_prefetch=1,
            grid=(TOK // rows,),
            in_specs=[whole] + [wide] * len(pieces),
            out_specs=whole,
        ),
        compiler_params=params(),
        cost_estimate=cost(0, 12 << 20),
        name="mix",
    )(pos, stepped, *pieces)


def per_device(queries, keys, values_in, out_grad, proj_local, outer_weight, momentum):
    r = lax.axis_index("replica")
    t = lax.axis_index("tensor")
    pos = jnp.stack([r // (NZ * 2), (r // 2) % NZ, r % 2, t // NL, t % NL]).astype(jnp.int32)
    weight = proj_local[0]

    to_core = split(pos, weight)
    grad_pieces = [out_grad] + [tensor_shift(out_grad, dy, dl) for dy, dl in SHIFTS[1:]]
    from_core = [replica_shift(p, 0, 0, 1) for p in to_core]
    from_x = [
        replica_shift(core_add(pos, weight, from_core[k], k), k, 0, 0) for k in range(1, NX)
    ]

    context = forward(queries, keys, values_in)
    terms = term(pos, context, weight)
    term_parts = [terms[0]] + [
        tensor_shift(p, dy, dl) for p, (dy, dl) in zip(terms[1:], SHIFTS[1:])
    ]

    own, *to_z = x_add(pos, weight, from_core[0], from_x)
    from_z = [replica_shift(to_z[j - 1], 0, j, 0) for j in range(1, NZ)]
    new_outer, new_momentum, half = outer_update(own, from_z, outer_weight, momentum)
    z_pieces = [half] + [replica_shift(half, 0, j, 0) for j in range(1, NZ)]
    x_own = jnp.concatenate(z_pieces, axis=1)
    x_pieces = [x_own] + [replica_shift(x_own, k, 0, 0) for k in range(1, NX)]
    c_pieces = [replica_shift(p, 0, 0, 1) for p in x_pieces]

    proj_grad, ctx_grad, square = grads(pos, grad_pieces, weight, context)
    square = square + tensor_shift(square, 0, 1)
    square = square + sum(tensor_shift(square, dy, 0) for dy in range(1, NY))
    query_grad, key_grad, value_grad = backward(queries, keys, values_in, ctx_grad)
    stepped = stepped_of(square, weight, proj_grad)

    attn_out = attn_sum(term_parts)
    new_local = mix(pos, stepped, x_pieces + c_pieces)
    return (attn_out, query_grad, key_grad, value_grad, new_local[None], new_outer, new_momentum)


def solution(mesh):
    return jax.shard_map(
        per_device,
        mesh=mesh,
        in_specs=(
            P("replica", "tensor"),
            P("replica", "tensor"),
            P("replica", "tensor"),
            P(("replica", "tensor"), None),
            P("replica", "tensor", None),
            P("tensor", "replica"),
            P("tensor", "replica"),
        ),
        out_specs=(
            P(("replica", "tensor"), None),
            P("replica", "tensor"),
            P("replica", "tensor"),
            P("replica", "tensor"),
            P("replica", "tensor", None),
            P("tensor", "replica"),
            P("tensor", "replica"),
        ),
        check_vma=False,
    )
```

```python
import functools

import jax
import jax.numpy as jnp
from jax import lax
from jax.experimental import pallas as pl
from jax.experimental.pallas import tpu as pltpu
from jax.sharding import PartitionSpec as P

D = 4096
HEADS = 32
KVH = 8
HD = 128
TOK = 512
ISLANDS = 32
GROUP = HEADS // KVH
NX = 4
NZ = 4
NY = 4
NL = 2
SHARE = 128
ROWS = 64

step_size = 0.02
mu_outer = 0.9
lr_outer = 0.7
mix_share = 0.5
eps_norm = 1e-06
scale_factor = HD ** (-0.5)

WHOLE = pl.BlockSpec(memory_space=pltpu.VMEM)
BF = jnp.bfloat16
F32 = jnp.float32
VMEM_LIMIT = 32 * 1024 * 1024


def params():
    return pltpu.CompilerParams(vmem_limit_bytes=VMEM_LIMIT)


def cost(flops, nbytes, trans=0):
    return pl.CostEstimate(flops=int(flops), bytes_accessed=int(nbytes), transcendentals=int(trans))


def kernel_call(kernel, outs, ins, in_specs, out_specs, name, estimate, grid=(), pos=None, scratch=(), after=(), alias=None):
    lead = 0 if pos is None else 1
    skip = len(after)

    def body(*refs):
        kernel(*refs[:lead], *refs[lead + skip :])

    specs = dict(
        grid=grid,
        in_specs=[pl.BlockSpec(memory_space=pl.ANY)] * skip + list(in_specs),
        out_specs=out_specs,
        scratch_shapes=list(scratch),
    )
    if pos is not None:
        specs = dict(grid_spec=pltpu.PrefetchScalarGridSpec(num_scalar_prefetch=1, **specs))
    lead_args = () if pos is None else (pos,)
    return pl.pallas_call(
        body,
        out_shape=outs,
        compiler_params=params(),
        cost_estimate=estimate,
        name=name,
        **specs,
    )(*lead_args, *after, *ins)


def array(*shape, dtype=None):
    return jax.ShapeDtypeStruct(shape, dtype or BF)


def replica_shift(v, dx, dz, dc):
    def at(x, z, c):
        return (x * NZ + z) * 2 + c

    pairs = [
        (at(x, z, c), at((x + dx) % NX, (z + dz) % NZ, (c + dc) % 2))
        for x in range(NX)
        for z in range(NZ)
        for c in range(2)
    ]
    return lax.ppermute(v, "replica", pairs)


def tensor_shift(v, dy, dl):
    pairs = [
        (y * NL + l, ((y + dy) % NY) * NL + (l + dl) % NL) for y in range(NY) for l in range(NL)
    ]
    return lax.ppermute(v, "tensor", pairs)


def tensor_swap(v):
    pairs = [(y * NL + l, (y ^ 1) * NL + l) for y in range(NY) for l in range(NL)]
    return lax.ppermute(v, "tensor", pairs)


def share_column(pos, dx, dz, dc):
    x, z, c = pos[0], pos[1], pos[2]
    return (((x + dx) % NX) * NZ + (z + dz) % NZ) * 2 + (c + dc) % 2


def token_block(pos, dy, dl):
    return ((pos[3] + dy) % NY) * NL + (pos[4] + dl) % NL


FIRST = slice(0, TOK // 2)
LAST = slice(TOK // 2, TOK)


CHUNKS = 8


def open_kernel(pos, w_hbm, g_hbm, w_ref, g_ref, send_ref, sems):
    rows = TOK // CHUNKS

    def here(i):
        return pl.ds(i * rows, rows)

    copies = [
        pltpu.make_async_copy(w_hbm.at[here(i)], w_ref.at[here(i)], sems.at[i])
        for i in range(CHUNKS)
    ] + [pltpu.make_async_copy(g_hbm, g_ref, sems.at[CHUNKS])]
    for copy in copies:
        copy.start()
    for i in range(CHUNKS):
        copies[i].wait()
        for k in range(NX):
            for j in range(NZ):
                at = pl.ds(pl.multiple_of(share_column(pos, k, j, 1) * SHARE, SHARE), SHARE)
                n = (k * NZ + j) * SHARE
                send_ref[i * rows : (i + 1) * rows, n : n + SHARE] = w_ref[
                    i * rows : (i + 1) * rows, at
                ]
    copies[CHUNKS].wait()


def open_step(pos, weight, out_grad):
    return kernel_call(
        open_kernel,
        [array(TOK, D), array(ROWS, D), array(TOK, D // 2)],
        (weight, out_grad),
        [pl.BlockSpec(memory_space=pl.ANY)] * 2,
        [WHOLE] * 3,
        "open_step",
        cost(0, 8 << 20),
        grid=(1,),
        pos=pos,
        scratch=[pltpu.SemaphoreType.DMA((CHUNKS + 1,))],
    )


def core_add_kernel(pos, w_ref, r_ref, own_ref, up_ref, down_ref, keep_ref):
    for rows, ks in ((FIRST, (0, 2, 3, 1)), (LAST, (0, 1, 2, 3))):
        for ref, k in zip((own_ref, up_ref, down_ref, keep_ref), ks):
            for j in range(NZ):
                at = pl.ds(pl.multiple_of(share_column(pos, k, j, 0) * SHARE, SHARE), SHARE)
                n = (k * NZ + j) * SHARE
                ref[rows, j * SHARE : (j + 1) * SHARE] = (
                    w_ref[rows, at].astype(F32) + r_ref[rows, n : n + SHARE].astype(F32)
                ).astype(BF)


def core_add(pos, weight, got, after):
    return kernel_call(
        core_add_kernel,
        [array(TOK, NZ * SHARE)] * 4,
        (weight, got),
        [WHOLE] * 2,
        [WHOLE] * 4,
        "core_add",
        cost(0, 6 << 20),
        grid=(1,),
        pos=pos,
        after=after,
    )


def ring_mid_kernel(keep_ref, low_ref, high_ref, up_ref, down_ref):
    up_ref[...] = (keep_ref[FIRST, :].astype(F32) + low_ref[FIRST, :].astype(F32)).astype(BF)
    down_ref[...] = (keep_ref[LAST, :].astype(F32) + high_ref[LAST, :].astype(F32)).astype(BF)


def ring_mid(keep, low, high, after=()):
    half = array(TOK // 2, keep.shape[1])
    return kernel_call(
        ring_mid_kernel,
        [half] * 2,
        (keep, low, high),
        [WHOLE] * 3,
        [WHOLE] * 2,
        "ring_mid",
        cost(0, keep.size * 6),
        after=after,
    )


def ring_total(own, low, high, low2, high2, rows, at):
    near, end = (high, low2) if rows == FIRST else (low, high2)
    total = own[rows, at].astype(F32) + near[rows, at].astype(F32)
    return total + end[:, at].astype(F32)


def x_add_kernel(own, low, high, low2, high2, own_ref, up_ref, down_ref, keep_ref):
    for rows, ks in ((FIRST, (0, 2, 3, 1)), (LAST, (0, 1, 2, 3))):
        for ref, j in zip((own_ref, up_ref, down_ref, keep_ref), ks):
            at = slice(j * SHARE, (j + 1) * SHARE)
            ref[rows, :] = ring_total(own, low, high, low2, high2, rows, at).astype(BF)


def x_add(parts, after=()):
    return kernel_call(
        x_add_kernel,
        [array(TOK, SHARE)] * 4,
        parts,
        [WHOLE] * 5,
        [WHOLE] * 4,
        "x_add",
        cost(0, 5 << 19),
        after=after,
    )


def outer_kernel(own, low, high, low2, high2, ow_ref, mo_ref, no_ref, nm_ref, nb_ref):
    for rows in (FIRST, LAST):
        total = ring_total(own, low, high, low2, high2, rows, slice(0, SHARE))
        outer = ow_ref[rows, :]
        delta = outer - total / ISLANDS
        moment = mu_outer * mo_ref[rows, :] + delta
        new = outer - lr_outer * (mu_outer * moment + delta)
        no_ref[rows, :] = new
        nm_ref[rows, :] = moment
        nb_ref[rows, :] = ((1.0 - mix_share) * new.astype(BF).astype(F32)).astype(BF)


def outer_update(parts, outer_weight, momentum, after):
    f32 = array(TOK, SHARE, dtype=F32)
    return kernel_call(
        outer_kernel,
        [f32, f32, array(TOK, SHARE)],
        (*parts, outer_weight, momentum),
        [WHOLE] * 7,
        [WHOLE] * 3,
        "outer_update",
        cost(0, 2 << 20),
        after=after,
    )


def cut_kernel(low_ref, high_ref, up_ref, down_ref):
    up_ref[...] = low_ref[FIRST, :]
    down_ref[...] = high_ref[LAST, :]


def cut(low, high, after=()):
    return kernel_call(
        cut_kernel,
        [array(TOK // 2, low.shape[1])] * 2,
        (low, high),
        [WHOLE] * 2,
        [WHOLE] * 2,
        "cut",
        cost(0, low.size * 4),
        after=after,
    )


def join_z_kernel(own, low, high, low2, high2, o_ref):
    o_ref[:, 0:SHARE] = own[...]
    o_ref[:, SHARE : 2 * SHARE] = low[...]
    o_ref[FIRST, 2 * SHARE : 3 * SHARE] = low2[...]
    o_ref[LAST, 2 * SHARE : 3 * SHARE] = high2[...]
    o_ref[:, 3 * SHARE : 4 * SHARE] = high[...]


def join_z(parts, after=()):
    return kernel_call(
        join_z_kernel,
        array(TOK, NZ * SHARE),
        parts,
        [WHOLE] * 5,
        WHOLE,
        "join_z",
        cost(0, 1 << 20),
        after=after,
    )


def hold_kernel(a_ref, o_ref):
    o_ref[...] = a_ref[...]


def hold(a, after):
    return kernel_call(
        hold_kernel,
        array(*a.shape),
        (a,),
        [WHOLE],
        WHOLE,
        "hold",
        cost(0, a.size * 4),
        after=after,
    )


def causal_mask(rows, cols, first):
    return lax.broadcasted_iota(jnp.int32, (rows, cols), 0) + first >= lax.broadcasted_iota(
        jnp.int32, (rows, cols), 1
    )


def dot(a, b, ca, cb):
    return lax.dot_general(a, b, (((ca,), (cb,)), ((), ())), preferred_element_type=F32)


def probs_of(q, k, first, rows, cols):
    scores = dot(q, k, 1, 1) * scale_factor
    scores = jnp.where(causal_mask(rows, cols, first), scores, -jnp.inf)
    highest = jnp.max(scores, axis=-1, keepdims=True)
    expon = jnp.exp(scores - highest)
    return expon / jnp.sum(expon, axis=-1, keepdims=True)


HALF = TOK // 2


def forward_kernel(q_ref, k_ref, v_ref, o_ref, t_ref):
    for part in range(2):
        first, cols = part * HALF, (part + 1) * HALF
        q = q_ref[first : first + HALF, :]
        probs = probs_of(q, k_ref[0:cols, :], first, HALF, cols)
        out = dot(probs.astype(BF), v_ref[0:cols, :], 1, 0).astype(BF)
        o_ref[first : first + HALF, :] = out
        t_ref[:, first : first + HALF] = out.T


def forward(queries, keys, values):
    head = pl.BlockSpec((TOK, HD), lambda h: (0, h))
    kv = pl.BlockSpec((TOK, HD), lambda h: (0, 0))
    return kernel_call(
        forward_kernel,
        [array(TOK, GROUP * HD), array(GROUP * HD, TOK)],
        (queries, keys, values),
        [head, kv, kv],
        [head, pl.BlockSpec((HD, TOK), lambda h: (h, 0))],
        "forward",
        cost(5e8, 2 << 20, 1 << 20),
        grid=(GROUP,),
    )


def backward_kernel(q_ref, k_ref, v_ref, g_ref, dq_ref, dk_ref, dv_ref, done_ref, dk_acc, dv_acc):
    h = pl.program_id(0)
    done_ref[...] = jnp.zeros_like(done_ref)

    @pl.when(h == 0)
    def _():
        dk_acc[...] = jnp.zeros_like(dk_acc)
        dv_acc[...] = jnp.zeros_like(dv_acc)

    for part in range(2):
        first, cols = part * HALF, (part + 1) * HALF
        rows = slice(first, first + HALF)
        q, g = q_ref[rows, :], g_ref[rows, :]
        k, v = k_ref[0:cols, :], v_ref[0:cols, :]
        probs = probs_of(q, k, first, HALF, cols)
        prob_grad = dot(g, v, 1, 1)
        inner = jnp.sum(prob_grad * probs, axis=-1, keepdims=True)
        score_grad = (probs * (prob_grad - inner) * scale_factor).astype(BF)
        dq_ref[rows, :] = dot(score_grad, k, 1, 0).astype(BF)
        dk_acc[0:cols, :] += dot(score_grad, q, 0, 0)
        dv_acc[0:cols, :] += dot(probs.astype(BF), g, 0, 0)

    @pl.when(h == GROUP - 1)
    def _():
        dk_ref[...] = dk_acc[...].astype(BF)
        dv_ref[...] = dv_acc[...].astype(BF)


def backward(queries, keys, values, ctx_grad, after):
    head = pl.BlockSpec((TOK, HD), lambda h: (0, h))
    kv = pl.BlockSpec((TOK, HD), lambda h: (0, 0))
    return kernel_call(
        backward_kernel,
        [array(TOK, GROUP * HD), array(TOK, HD), array(TOK, HD), array(8, 128, dtype=F32)],
        (queries, keys, values, ctx_grad),
        [head, kv, kv, head],
        [head, kv, kv, WHOLE],
        "backward",
        cost(1.3e9, 3 << 20, 1 << 20),
        grid=(GROUP,),
        scratch=[pltpu.VMEM((TOK, HD), F32), pltpu.VMEM((TOK, HD), F32)],
        after=after,
    )


TILE = 512


HALF_ROWS = ROWS // 2


def term_kernel(
    pos, c_ref, w_ref, up_ref, down_ref, keep_up_ref, keep_down_ref, own_ref, mate_ref, held
):
    at = pl.ds(pl.multiple_of(pl.program_id(0) * TILE, TILE), TILE)
    held[...] = dot(c_ref[...], w_ref[:, at], 1, 0).astype(BF)

    def rows(dy, dl, first=0, count=ROWS):
        row = pl.multiple_of(token_block(pos, dy, dl) * ROWS + first, HALF_ROWS)
        return held[pl.ds(row, count), :]

    for dl in range(NL):
        low = slice(dl * HALF_ROWS, (dl + 1) * HALF_ROWS)
        up_ref[low, at] = rows(2, dl, 0, HALF_ROWS)
        down_ref[low, at] = rows(2, dl, HALF_ROWS, HALF_ROWS)
        full = slice(dl * ROWS, (dl + 1) * ROWS)
        keep_up_ref[full, at] = rows(1, dl)
        keep_down_ref[full, at] = rows(3, dl)
    own_ref[:, at] = rows(0, 0)
    mate_ref[:, at] = rows(0, 1)


def term(pos, context, weight, after):
    return kernel_call(
        term_kernel,
        [array(ROWS, D)] * 2 + [array(2 * ROWS, D)] * 2 + [array(ROWS, D)] * 2,
        (context, weight),
        [WHOLE, WHOLE],
        [WHOLE] * 6,
        "term",
        cost(2.1e9, 9 << 20),
        grid=(D // TILE,),
        pos=pos,
        scratch=[pltpu.VMEM((TOK, TILE), BF)],
        after=after,
    )


def term_mid_kernel(keep_up_ref, keep_down_ref, low_ref, high_ref, up_ref, down_ref):
    for dl in range(NL):
        part = slice(dl * HALF_ROWS, (dl + 1) * HALF_ROWS)
        first = slice(dl * ROWS, dl * ROWS + HALF_ROWS)
        last = slice(dl * ROWS + HALF_ROWS, (dl + 1) * ROWS)
        up_ref[first, :] = (
            keep_up_ref[first, :].astype(F32) + low_ref[part, :].astype(F32)
        ).astype(BF)
        up_ref[last, :] = keep_up_ref[last, :]
        down_ref[first, :] = keep_down_ref[first, :]
        down_ref[last, :] = (
            keep_down_ref[last, :].astype(F32) + high_ref[part, :].astype(F32)
        ).astype(BF)


def term_mid(keep_up, keep_down, low, high, after):
    return kernel_call(
        term_mid_kernel,
        [array(2 * ROWS, D)] * 2,
        (keep_up, keep_down, low, high),
        [WHOLE] * 4,
        [WHOLE] * 2,
        "term_mid",
        cost(0, 5 << 20),
        after=after,
    )


def sum_kernel(own_ref, up_ref, down_ref, mate_ref, o_ref):
    total = own_ref[...].astype(F32) + up_ref[0:ROWS, :].astype(F32)
    total = total + down_ref[0:ROWS, :].astype(F32)
    o_ref[...] = (total + mate_ref[...].astype(F32)).astype(BF)


def mate_kernel(mate_ref, up_ref, down_ref, o_ref):
    total = mate_ref[...].astype(F32) + up_ref[ROWS : 2 * ROWS, :].astype(F32)
    o_ref[...] = (total + down_ref[ROWS : 2 * ROWS, :].astype(F32)).astype(BF)


def row_sum(kernel, name, *parts, after=()):
    return kernel_call(
        kernel,
        array(ROWS, D),
        parts,
        [WHOLE] * len(parts),
        WHOLE,
        name,
        cost(0, ROWS * D * 2 * (len(parts) + 1)),
        after=after,
    )


def relay_kernel(own_low, own_high, mate_low, mate_high, up_ref, down_ref):
    for n, (low, high) in enumerate(((own_low, own_high), (mate_low, mate_high))):
        part = slice(n * HALF_ROWS, (n + 1) * HALF_ROWS)
        up_ref[part, :] = low[0:HALF_ROWS, :]
        down_ref[part, :] = high[HALF_ROWS:ROWS, :]


def relay(parts, after):
    return kernel_call(
        relay_kernel,
        [array(ROWS, D)] * 2,
        parts,
        [WHOLE] * 4,
        [WHOLE] * 2,
        "relay",
        cost(0, 2 << 20),
        after=after,
    )


def add_kernel(a_ref, b_ref, o_ref):
    o_ref[...] = a_ref[...] + b_ref[...]


def add_small(a, b, after):
    return kernel_call(
        add_kernel,
        array(8, 128, dtype=F32),
        (a, b),
        [WHOLE] * 2,
        WHOLE,
        "add_small",
        cost(0, 1 << 14),
        after=after,
    )


def grads_kernel(pos, *refs, last):
    pieces, w_ref, t_ref, rest = refs[:8], refs[8], refs[9], refs[10:]
    if last:
        acc_in, sq_in, proj_ref, ctx_ref, sq_ref, held, acc, sq = rest
    else:
        proj_ref, ctx_ref, sq_ref, held, acc, sq = rest
    i = pl.program_id(0)

    @pl.when(i == 0)
    def _():
        acc[...] = acc_in[...] if last else jnp.zeros_like(acc)
        sq[...] = sq_in[...] if last else jnp.zeros_like(sq)

    def place(dy, dl, piece, first=0):
        row = pl.multiple_of(token_block(pos, dy, dl) * ROWS + first, HALF_ROWS)
        held[pl.ds(row, piece.shape[0]), :] = piece

    for n, (dy, dl) in enumerate(((0, 0), (0, 1), (-1, 0), (-1, 1), (1, 0), (1, 1))):
        place(dy, dl, pieces[n][...])
    for dl in range(NL):
        part = slice(dl * HALF_ROWS, (dl + 1) * HALF_ROWS)
        place(2, dl, pieces[6][part, :])
        place(2, dl, pieces[7][part, :], HALF_ROWS)
    at = pl.ds(pl.multiple_of((i + (D // TILE // 2 if last else 0)) * TILE, TILE), TILE)
    grad = held[...]
    acc[...] += dot(grad, w_ref[:, at], 1, 1)
    proj = dot(t_ref[...], grad, 1, 0)
    proj_ref[...] = proj.astype(BF)
    sq[...] += jnp.sum((proj * proj).reshape(TOK // 8, 8, TILE), axis=0)

    @pl.when(i == pl.num_programs(0) - 1)
    def _():
        ctx_ref[...] = acc[...].astype(ctx_ref.dtype)
        if last:
            sq_ref[...] = jnp.broadcast_to(jnp.sum(sq[...], axis=(0, 1), keepdims=True), (8, 128))
        else:
            sq_ref[...] = sq[...]


def grads(pos, pieces, weight, turned, carry, after):
    hq = GROUP * HD
    last = bool(carry)
    steps = D // TILE // 2
    start = steps if last else 0

    def tile(rows):
        return pl.BlockSpec((rows, TILE), lambda i, pos: (0, start + i))

    return kernel_call(
        functools.partial(grads_kernel, last=last),
        [
            array(hq, D // 2),
            array(TOK, hq, dtype=BF if last else F32),
            array(8, 128 if last else TILE, dtype=F32),
        ],
        (*pieces, weight, turned, *carry),
        [tile(ROWS)] * 8 + [WHOLE] * (2 + len(carry)),
        [pl.BlockSpec((hq, TILE), lambda i, pos: (0, i)), WHOLE, WHOLE],
        "grads_last" if last else "grads_first",
        cost(2.2e9, 7 << 20),
        grid=(steps,),
        pos=pos,
        scratch=[
            pltpu.VMEM((TOK, TILE), BF),
            pltpu.VMEM((TOK, hq), F32),
            pltpu.VMEM((8, TILE), F32),
        ],
        after=after,
    )


def stepped_kernel(sq_ref, more_ref, w_ref, a_ref, b_ref, o_ref):
    square = sq_ref[0:1, 0:1] + more_ref[0:1, 0:1]
    rate = step_size / jnp.sqrt(square / (HEADS * HD * D) + eps_norm)
    for n, ref in enumerate((a_ref, b_ref)):
        at = slice(n * D // 2, (n + 1) * D // 2)
        stepped = (w_ref[:, at].astype(F32) - rate * ref[...].astype(F32)).astype(BF)
        o_ref[:, at] = (mix_share * stepped.astype(F32)).astype(BF)


def stepped_of(square, more, weight, proj, after):
    rows = 64
    spec = pl.BlockSpec((rows, D), lambda i: (i, 0))
    half = pl.BlockSpec((rows, D // 2), lambda i: (i, 0))
    return kernel_call(
        stepped_kernel,
        array(TOK, D),
        (square, more, weight, *proj),
        [WHOLE, WHOLE, spec, half, half],
        spec,
        "stepped",
        cost(0, 12 << 20),
        grid=(TOK // rows,),
        after=after,
    )


def mix_kernel(pos, s_ref, *refs):
    pieces, (o_hbm, held, sems) = refs[:-3], refs[-3:]
    rows = TOK // CHUNKS
    copies = []
    for i in range(CHUNKS):
        here = slice(i * rows, (i + 1) * rows)
        n = 0
        for c in range(2):
            for k in range(NX):
                if k == 2:
                    piece = pieces[n + i // (CHUNKS // 2)]
                    there = slice(i % (CHUNKS // 2) * rows, (i % (CHUNKS // 2) + 1) * rows)
                    n += 2
                else:
                    piece, there = pieces[n], here
                    n += 1
                for j in range(NZ):
                    at = pl.ds(pl.multiple_of(share_column(pos, -k, -j, c) * SHARE, SHARE), SHARE)
                    held[here, at] = s_ref[here, at] + piece[there, j * SHARE : (j + 1) * SHARE]
        copies.append(pltpu.make_async_copy(held.at[here], o_hbm.at[here], sems.at[i]))
        copies[-1].start()
    for copy in copies:
        copy.wait()


def mix(pos, stepped, pieces):
    return kernel_call(
        mix_kernel,
        array(TOK, D),
        (stepped, *pieces),
        [WHOLE] * (1 + len(pieces)),
        pl.BlockSpec(memory_space=pl.ANY),
        "mix",
        cost(0, 12 << 20),
        grid=(1,),
        pos=pos,
        scratch=[pltpu.VMEM((TOK, D), BF), pltpu.SemaphoreType.DMA((CHUNKS,))],
    )


def per_device(queries, keys, values_in, out_grad, proj_local, outer_weight, momentum):
    r = lax.axis_index("replica")
    t = lax.axis_index("tensor")
    pos = jnp.stack([r // (NZ * 2), (r // 2) % NZ, r % 2, t // NL, t % NL]).astype(jnp.int32)

    def x_shift(v, d):
        return replica_shift(v, d % NX, 0, 0)

    def z_shift(v, d):
        return replica_shift(v, 0, d % NZ, 0)

    def y_shift(v, d):
        return tensor_shift(v, d % NY, 0)

    def mate_shift(v):
        return tensor_shift(v, 0, 1)

    def core_swap(v):
        return replica_shift(v, 0, 0, 1)

    weight, grad_own, send = open_step(pos, proj_local[0], out_grad)
    from_core = core_swap(send)
    grad_mate = mate_shift(grad_own)
    own_low, own_high = y_shift(grad_own, 1), y_shift(grad_own, -1)
    context, turned = forward(queries, keys, values_in)

    x_own, x_up, x_down, x_keep = core_add(pos, weight, from_core, (context,))
    x_low, x_high = x_shift(x_up, 1), x_shift(x_down, -1)
    grad_mate = hold(grad_mate, (x_up,))
    mate_low, mate_high = y_shift(grad_mate, 1), y_shift(grad_mate, -1)

    x_up2, x_down2 = ring_mid(x_keep, x_low, x_high, (grad_mate,))
    x_low2, x_high2 = x_shift(x_up2, 1), x_shift(x_down2, -1)
    relay_up, relay_down = relay((own_low, own_high, mate_low, mate_high), (x_up2,))
    relay_low, relay_high = y_shift(relay_up, 1), y_shift(relay_down, -1)
    z_own, z_up, z_down, z_keep = x_add((x_own, x_low, x_high, x_low2, x_high2), (relay_up,))
    z_low, z_high = z_shift(z_up, 1), z_shift(z_down, -1)

    send_up, send_down, keep_up, keep_down, kept_own, kept_mate = term(
        pos, context, weight, (z_up,)
    )
    term_low, term_high = y_shift(send_up, 1), y_shift(send_down, -1)
    z_up2, z_down2 = ring_mid(z_keep, z_low, z_high, (send_up,))
    z_low2, z_high2 = z_shift(z_up2, 1), z_shift(z_down2, -1)

    pieces = (
        grad_own, grad_mate, own_low, mate_low, own_high, mate_high, relay_low, relay_high
    )
    proj_a, acc, sq = grads(pos, pieces, weight, turned, (), (z_up2,))
    new_outer, new_momentum, half = outer_update(
        (z_own, z_low, z_high, z_low2, z_high2), outer_weight, momentum, (sq,)
    )
    o_low, o_high = z_shift(half, 1), z_shift(half, -1)
    proj_b, ctx_grad, square = grads(pos, pieces, weight, turned, (acc, sq), (half,))
    square_mate = mate_shift(square)
    send_up2, send_down2 = term_mid(keep_up, keep_down, term_low, term_high, (square,))
    term_low2, term_high2 = y_shift(send_up2, 1), y_shift(send_down2, -1)
    o_up2, o_down2 = cut(o_low, o_high, (send_up2,))
    o_low2, o_high2 = z_shift(o_up2, 1), z_shift(o_down2, -1)
    square = add_small(square, square_mate, (o_up2,))
    square_next = tensor_swap(square)
    query_grad, key_grad, value_grad, done = backward(queries, keys, values_in, ctx_grad, (square,))

    group = join_z((half, o_low, o_high, o_low2, o_high2), (done,))
    g_low, g_high = x_shift(group, 1), x_shift(group, -1)
    square = add_small(square, square_next, (group,))
    more = tensor_shift(square, 2, 0)
    send_mate = row_sum(mate_kernel, "mate_sum", kept_mate, term_low2, term_high2, after=(square,))
    term_mate = mate_shift(send_mate)
    stepped = stepped_of(square, more, weight, (proj_a, proj_b), (send_mate,))
    g_up2, g_down2 = cut(g_low, g_high, (stepped,))
    g_low2, g_high2 = x_shift(g_up2, 1), x_shift(g_down2, -1)
    attn_out = row_sum(
        sum_kernel, "attn_sum", kept_own, term_low2, term_high2, term_mate, after=(g_up2,)
    )
    x_pieces = [group, g_low, g_low2, g_high2, g_high]
    c_pieces = [core_swap(p) for p in x_pieces]
    new_local = mix(pos, stepped, x_pieces + c_pieces)
    return (attn_out, query_grad, key_grad, value_grad, new_local[None], new_outer, new_momentum)


def solution(mesh):
    return jax.shard_map(
        per_device,
        mesh=mesh,
        in_specs=(
            P("replica", "tensor"),
            P("replica", "tensor"),
            P("replica", "tensor"),
            P(("replica", "tensor"), None),
            P("replica", "tensor", None),
            P("tensor", "replica"),
            P("tensor", "replica"),
        ),
        out_specs=(
            P(("replica", "tensor"), None),
            P("replica", "tensor"),
            P("replica", "tensor"),
            P("replica", "tensor"),
            P("replica", "tensor", None),
            P("tensor", "replica"),
            P("tensor", "replica"),
        ),
        check_vma=False,
    )
```

```python
import functools

import jax
import jax.numpy as jnp
from jax import lax
from jax.experimental import pallas as pl
from jax.experimental.pallas import tpu as pltpu
from jax.sharding import PartitionSpec as P

D = 4096
HEADS = 32
KVH = 8
HD = 128
TOK = 512
ISLANDS = 32
GROUP = HEADS // KVH
NX = 4
NZ = 4
NY = 4
NL = 2
SHARE = 128
ROWS = 64

step_size = 0.02
mu_outer = 0.9
lr_outer = 0.7
mix_share = 0.5
eps_norm = 1e-06
scale_factor = HD ** (-0.5)

WHOLE = pl.BlockSpec(memory_space=pltpu.VMEM)
BF = jnp.bfloat16
F32 = jnp.float32
VMEM_LIMIT = 32 * 1024 * 1024


def params():
    return pltpu.CompilerParams(vmem_limit_bytes=VMEM_LIMIT)


def cost(flops, nbytes, trans=0):
    return pl.CostEstimate(
        flops=int(flops * 0.25), bytes_accessed=int(nbytes * 0.25), transcendentals=int(trans * 0.25)
    )


def kernel_call(kernel, outs, ins, in_specs, out_specs, name, estimate, grid=(), pos=None, scratch=(), after=(), alias=None):
    lead = 0 if pos is None else 1
    skip = len(after)

    def body(*refs):
        kernel(*refs[:lead], *refs[lead + skip :])

    specs = dict(
        grid=grid,
        in_specs=[pl.BlockSpec(memory_space=pl.ANY)] * skip + list(in_specs),
        out_specs=out_specs,
        scratch_shapes=list(scratch),
    )
    if pos is not None:
        specs = dict(grid_spec=pltpu.PrefetchScalarGridSpec(num_scalar_prefetch=1, **specs))
    lead_args = () if pos is None else (pos,)
    return pl.pallas_call(
        body,
        out_shape=outs,
        compiler_params=params(),
        cost_estimate=estimate,
        name=name,
        input_output_aliases=alias or {},
        **specs,
    )(*lead_args, *after, *ins)


def array(*shape, dtype=None):
    return jax.ShapeDtypeStruct(shape, dtype or BF)


def replica_shift(v, dx, dz, dc):
    def at(x, z, c):
        return (x * NZ + z) * 2 + c

    pairs = [
        (at(x, z, c), at((x + dx) % NX, (z + dz) % NZ, (c + dc) % 2))
        for x in range(NX)
        for z in range(NZ)
        for c in range(2)
    ]
    return lax.ppermute(v, "replica", pairs)


def tensor_shift(v, dy, dl):
    pairs = [
        (y * NL + l, ((y + dy) % NY) * NL + (l + dl) % NL) for y in range(NY) for l in range(NL)
    ]
    return lax.ppermute(v, "tensor", pairs)


def tensor_swap(v):
    pairs = [(y * NL + l, (y ^ 1) * NL + l) for y in range(NY) for l in range(NL)]
    return lax.ppermute(v, "tensor", pairs)


def share_column(pos, dx, dz, dc):
    x, z, c = pos[0], pos[1], pos[2]
    return (((x + dx) % NX) * NZ + (z + dz) % NZ) * 2 + (c + dc) % 2


def token_block(pos, dy, dl):
    return ((pos[3] + dy) % NY) * NL + (pos[4] + dl) % NL


FIRST = slice(0, TOK // 2)
LAST = slice(TOK // 2, TOK)


CHUNKS = 8


def open_kernel(pos, w_ref, send_ref):
    for k in range(NX):
        for j in range(NZ):
            at = pl.ds(pl.multiple_of(share_column(pos, k, j, 1) * SHARE, SHARE), SHARE)
            n = (k * NZ + j) * SHARE
            send_ref[:, n : n + SHARE] = w_ref[:, at]


def open_step(pos, weight):
    return kernel_call(
        open_kernel,
        array(TOK, D // 2),
        (weight,),
        [WHOLE],
        WHOLE,
        "open_step",
        cost(0, 8 << 20),
        grid=(1,),
        pos=pos,
    )


def core_add_kernel(pos, w_ref, r_ref, own_ref, up_ref, down_ref, keep_ref):
    for rows, ks in ((FIRST, (0, 2, 3, 1)), (LAST, (0, 1, 2, 3))):
        for ref, k in zip((own_ref, up_ref, down_ref, keep_ref), ks):
            for j in range(NZ):
                at = pl.ds(pl.multiple_of(share_column(pos, k, j, 0) * SHARE, SHARE), SHARE)
                n = (k * NZ + j) * SHARE
                ref[rows, j * SHARE : (j + 1) * SHARE] = (
                    w_ref[rows, at].astype(F32) + r_ref[rows, n : n + SHARE].astype(F32)
                ).astype(BF)


def core_add(pos, weight, got, after):
    return kernel_call(
        core_add_kernel,
        [array(TOK, NZ * SHARE)] * 4,
        (weight, got),
        [WHOLE] * 2,
        [WHOLE] * 4,
        "core_add",
        cost(0, 6 << 20),
        grid=(1,),
        pos=pos,
        after=after,
    )


def ring_mid_kernel(keep_ref, low_ref, high_ref, up_ref, down_ref):
    up_ref[...] = (keep_ref[FIRST, :].astype(F32) + low_ref[FIRST, :].astype(F32)).astype(BF)
    down_ref[...] = (keep_ref[LAST, :].astype(F32) + high_ref[LAST, :].astype(F32)).astype(BF)


def ring_mid(keep, low, high, after=()):
    half = array(TOK // 2, keep.shape[1])
    return kernel_call(
        ring_mid_kernel,
        [half] * 2,
        (keep, low, high),
        [WHOLE] * 3,
        [WHOLE] * 2,
        "ring_mid",
        cost(0, keep.size * 6),
        after=after,
    )


def ring_total(own, low, high, low2, high2, rows, at):
    near, end = (high, low2) if rows == FIRST else (low, high2)
    total = own[rows, at].astype(F32) + near[rows, at].astype(F32)
    return total + end[:, at].astype(F32)


def x_add_kernel(own, low, high, low2, high2, *outs):
    for rows in (FIRST, LAST):
        for j, ref in enumerate(outs):
            at = slice(j * SHARE, (j + 1) * SHARE)
            ref[rows, :] = ring_total(own, low, high, low2, high2, rows, at).astype(BF)


def x_add(parts, after=()):
    return kernel_call(
        x_add_kernel,
        [array(TOK, SHARE)] * 4,
        parts,
        [WHOLE] * 5,
        [WHOLE] * 4,
        "x_add",
        cost(0, 5 << 19),
        after=after,
    )


def outer_kernel(own, one, two, three, ow_ref, mo_ref, no_ref, nm_ref, nb_ref):
    total = own[...].astype(F32) + one[...].astype(F32)
    total = total + two[...].astype(F32)
    total = total + three[...].astype(F32)
    outer = ow_ref[...]
    delta = outer - total / ISLANDS
    moment = mu_outer * mo_ref[...] + delta
    new = outer - lr_outer * (mu_outer * moment + delta)
    no_ref[...] = new
    nm_ref[...] = moment
    nb_ref[...] = ((1.0 - mix_share) * new.astype(BF).astype(F32)).astype(BF)


def outer_update(parts, outer_weight, momentum, after):
    f32 = array(TOK, SHARE, dtype=F32)
    return kernel_call(
        outer_kernel,
        [f32, f32, array(TOK, SHARE)],
        (*parts, outer_weight, momentum),
        [WHOLE] * 6,
        [WHOLE] * 3,
        "outer_update",
        cost(0, 2 << 20),
        after=after,
    )


def cut_kernel(low_ref, high_ref, up_ref, down_ref):
    up_ref[...] = low_ref[FIRST, :]
    down_ref[...] = high_ref[LAST, :]


def cut(low, high, after=()):
    return kernel_call(
        cut_kernel,
        [array(TOK // 2, low.shape[1])] * 2,
        (low, high),
        [WHOLE] * 2,
        [WHOLE] * 2,
        "cut",
        cost(0, low.size * 4),
        after=after,
    )


def join_z_kernel(*refs):
    for j, ref in enumerate(refs[:-1]):
        refs[-1][:, j * SHARE : (j + 1) * SHARE] = ref[...]


def join_z(parts, after=()):
    return kernel_call(
        join_z_kernel,
        array(TOK, NZ * SHARE),
        parts,
        [WHOLE] * NZ,
        WHOLE,
        "join_z",
        cost(0, 1 << 20),
        after=after,
    )


def stack_kernel(*refs):
    start = 0
    for ref in refs[:-1]:
        rows = ref.shape[0]
        refs[-1][start : start + rows, :] = ref[...]
        start += rows


def stack(parts, after=()):
    rows, columns = sum(p.shape[0] for p in parts), parts[0].shape[1]
    return kernel_call(
        stack_kernel,
        array(rows, columns),
        parts,
        [WHOLE] * len(parts),
        WHOLE,
        "stack",
        cost(0, rows * columns * 4),
        after=after,
    )


def hold_kernel(a_ref, o_ref):
    o_ref[...] = a_ref[...]


def hold(a, after):
    return kernel_call(
        hold_kernel,
        array(*a.shape),
        (a,),
        [WHOLE],
        WHOLE,
        "hold",
        cost(0, a.size * 4),
        after=after,
    )


POWER = scale_factor * 1.4426950408889634


def dot(a, b, ca, cb):
    return lax.dot_general(a, b, (((ca,), (cb,)), ((), ())), preferred_element_type=F32)


def probs_of(q, k):
    scores = dot(k, q, 1, 1)
    shape = scores.shape
    causal = lax.broadcasted_iota(jnp.int32, shape, 0) <= lax.broadcasted_iota(jnp.int32, shape, 1)
    scores = jnp.where(causal, scores, -jnp.inf)
    highest = jnp.max(scores, axis=0, keepdims=True)
    expon = jnp.exp2(scores * POWER - highest * POWER)
    return expon * (1.0 / jnp.sum(expon, axis=0, keepdims=True))


def forward_kernel(q_ref, k_ref, v_ref, o_ref, t_ref):
    turned = v_ref[...].T
    for h in range(GROUP):
        head = slice(h * HD, (h + 1) * HD)
        probs = probs_of(q_ref[:, head], k_ref[...]).astype(BF)
        out = dot(turned, probs, 1, 0).astype(BF)
        t_ref[head, :] = out
        o_ref[:, head] = out.T


def forward(queries, keys, values, after):
    return kernel_call(
        forward_kernel,
        [array(TOK, GROUP * HD), array(GROUP * HD, TOK)],
        (queries, keys, values),
        [WHOLE] * 3,
        [WHOLE] * 2,
        "forward",
        cost(5e8, 2 << 20, 1 << 20),
        after=after,
    )


def backward_kernel(q_ref, k_ref, v_ref, g_ref, dq_ref, dk_ref, dv_ref, done_ref):
    done_ref[...] = jnp.zeros_like(done_ref)
    key_grad = jnp.zeros((TOK, HD), F32)
    value_grad = jnp.zeros((TOK, HD), F32)
    k, v = k_ref[...], v_ref[...]
    for h in range(GROUP):
        head = slice(h * HD, (h + 1) * HD)
        q, g = q_ref[:, head], g_ref[:, head]
        probs = probs_of(q, k)
        prob_grad = dot(v, g, 1, 1)
        inner = jnp.sum(prob_grad * probs, axis=0, keepdims=True)
        score_grad = (probs * (prob_grad - inner) * scale_factor).astype(BF)
        dq_ref[:, head] = dot(score_grad, k, 0, 0).astype(BF)
        key_grad += dot(score_grad, q, 1, 0)
        value_grad += dot(probs.astype(BF), g, 1, 0)
    dk_ref[...] = key_grad.astype(BF)
    dv_ref[...] = value_grad.astype(BF)


def backward(queries, keys, values, ctx_grad, after):
    return kernel_call(
        backward_kernel,
        [array(TOK, GROUP * HD), array(TOK, HD), array(TOK, HD), array(8, 128, dtype=F32)],
        (queries, keys, values, ctx_grad),
        [WHOLE] * 4,
        [WHOLE] * 4,
        "backward",
        cost(1.3e9, 400 << 20, 1 << 20),
        after=after,
    )


TILE = 512


HALF_ROWS = ROWS // 2


def term_kernel(
    pos, c_ref, w_ref, up_ref, down_ref, keep_up_ref, keep_down_ref, own_ref, mate_ref, held
):
    at = pl.ds(pl.multiple_of(pl.program_id(0) * TILE, TILE), TILE)
    held[...] = dot(c_ref[...], w_ref[:, at], 1, 0).astype(BF)

    def rows(dy, dl, first=0, count=ROWS):
        row = pl.multiple_of(token_block(pos, dy, dl) * ROWS + first, HALF_ROWS)
        return held[pl.ds(row, count), :]

    for dl in range(NL):
        low = slice(dl * HALF_ROWS, (dl + 1) * HALF_ROWS)
        up_ref[low, at] = rows(2, dl, 0, HALF_ROWS)
        down_ref[low, at] = rows(2, dl, HALF_ROWS, HALF_ROWS)
        full = slice(dl * ROWS, (dl + 1) * ROWS)
        keep_up_ref[full, at] = rows(1, dl)
        keep_down_ref[full, at] = rows(3, dl)
    own_ref[:, at] = rows(0, 0)
    mate_ref[:, at] = rows(0, 1)


def term(pos, context, weight, after):
    return kernel_call(
        term_kernel,
        [array(ROWS, D)] * 2 + [array(2 * ROWS, D)] * 2 + [array(ROWS, D)] * 2,
        (context, weight),
        [WHOLE, WHOLE],
        [WHOLE] * 6,
        "term",
        cost(2.1e9, 9 << 20),
        grid=(D // TILE,),
        pos=pos,
        scratch=[pltpu.VMEM((TOK, TILE), BF)],
        after=after,
    )


PAD = 128
WIDE = D + PAD


def get_square(ref):
    return ref[0:16, D:WIDE].astype(F32) + ref[16:32, D:WIDE].astype(F32)


def term_mid_kernel(keep_up_ref, keep_down_ref, low_ref, high_ref, sq_ref, up_ref, down_ref):
    square = jnp.concatenate([sq_ref[...]] * 2, axis=0)
    high = square.astype(BF)
    for ref in (up_ref, down_ref):
        ref[:, D:WIDE] = jnp.zeros((2 * ROWS, PAD), BF)
        ref[0:16, D:WIDE] = high
        ref[16:32, D:WIDE] = (square - high.astype(F32)).astype(BF)
    for dl in range(NL):
        part = slice(ROWS + dl * HALF_ROWS, ROWS + (dl + 1) * HALF_ROWS)
        first = slice(dl * ROWS, dl * ROWS + HALF_ROWS)
        last = slice(dl * ROWS + HALF_ROWS, (dl + 1) * ROWS)
        up_ref[first, 0:D] = (
            keep_up_ref[first, :].astype(F32) + low_ref[part, :].astype(F32)
        ).astype(BF)
        up_ref[last, 0:D] = keep_up_ref[last, :]
        down_ref[first, 0:D] = keep_down_ref[first, :]
        down_ref[last, 0:D] = (
            keep_down_ref[last, :].astype(F32) + high_ref[part, :].astype(F32)
        ).astype(BF)


def term_mid(parts, after):
    return kernel_call(
        term_mid_kernel,
        [array(2 * ROWS, WIDE)] * 2,
        parts,
        [WHOLE] * 5,
        [WHOLE] * 2,
        "term_mid",
        cost(0, 5 << 20),
        after=after,
    )


def sum_kernel(own_ref, up_ref, down_ref, mate_ref, o_ref):
    total = own_ref[...].astype(F32) + up_ref[0:ROWS, 0:D].astype(F32)
    total = total + down_ref[0:ROWS, 0:D].astype(F32)
    o_ref[...] = (total + mate_ref[...].astype(F32)).astype(BF)


def mate_kernel(mate_ref, up_ref, down_ref, o_ref):
    total = mate_ref[...].astype(F32) + up_ref[ROWS : 2 * ROWS, 0:D].astype(F32)
    o_ref[...] = (total + down_ref[ROWS : 2 * ROWS, 0:D].astype(F32)).astype(BF)


def row_sum(kernel, name, *parts, after=(), weigh=1, token=False):
    more = [array(8, 128, dtype=F32)] if token else []
    outs = kernel_call(
        kernel,
        [array(ROWS, D)] + more,
        parts,
        [WHOLE] * len(parts),
        [WHOLE] * (1 + len(more)),
        name,
        cost(0, weigh * ROWS * D * 2 * (len(parts) + 1)),
        after=after,
    )
    return outs if token else outs[0]


def relay_kernel(
    own_low, own_high, mate_low, mate_high, term_up, term_down, up_ref, down_ref
):
    for n, (low, high) in enumerate(((own_low, own_high), (mate_low, mate_high))):
        part = slice(n * HALF_ROWS, (n + 1) * HALF_ROWS)
        up_ref[part, :] = low[0:HALF_ROWS, :]
        down_ref[part, :] = high[HALF_ROWS:ROWS, :]
    up_ref[ROWS : 2 * ROWS, :] = term_up[...]
    down_ref[ROWS : 2 * ROWS, :] = term_down[...]


def relay(parts, after):
    return kernel_call(
        relay_kernel,
        [array(2 * ROWS, D)] * 2,
        parts,
        [WHOLE] * 6,
        [WHOLE] * 2,
        "relay",
        cost(0, 4 << 20),
        after=after,
    )


def add_kernel(a_ref, b_ref, o_ref):
    o_ref[...] = a_ref[...] + b_ref[...]


def add_small(a, b, after):
    return kernel_call(
        add_kernel,
        array(8, 128, dtype=F32),
        (a, b),
        [WHOLE] * 2,
        WHOLE,
        "add_small",
        cost(0, 1 << 14),
        after=after,
    )


def grads_kernel(pos, *refs):
    pieces, (w_ref, t_ref, proj_ref, ctx_ref, sq_ref, held) = refs[:8], refs[8:]

    def place(dy, dl, piece, first=0):
        row = pl.multiple_of(token_block(pos, dy, dl) * ROWS + first, HALF_ROWS)
        held[pl.ds(row, piece.shape[0]), :] = piece

    for n, (dy, dl) in enumerate(((0, 0), (0, 1), (-1, 0), (-1, 1), (1, 0), (1, 1))):
        place(dy, dl, pieces[n][...])
    for dl in range(NL):
        part = slice(dl * HALF_ROWS, (dl + 1) * HALF_ROWS)
        place(2, dl, pieces[6][part, :])
        place(2, dl, pieces[7][part, :], HALF_ROWS)

    ctx_ref[...] = dot(held[...], w_ref[...], 1, 1).astype(BF)
    turned = t_ref[...]
    square = jnp.zeros((8, TILE), F32)
    for i in range(D // TILE):
        at = slice(i * TILE, (i + 1) * TILE)
        proj = dot(turned, held[:, at], 1, 0)
        proj_ref[:, at] = proj.astype(BF)
        square += jnp.sum((proj * proj).reshape(TOK // 8, 8, TILE), axis=0)
    sq_ref[...] = jnp.broadcast_to(jnp.sum(square, axis=(0, 1), keepdims=True), (8, 128))


def grads(pos, pieces, weight, turned, after):
    hq = GROUP * HD
    return kernel_call(
        grads_kernel,
        [array(hq, D), array(TOK, hq), array(8, 128, dtype=F32)],
        (*pieces, weight, turned),
        [WHOLE] * 10,
        [WHOLE] * 3,
        "grads",
        cost(4.3e9, 13 << 20),
        grid=(1,),
        pos=pos,
        scratch=[pltpu.VMEM((TOK, D), BF)],
        after=after,
    )


BLOCK = D // NX


def block_columns(pos, k, j, c):
    here = pl.multiple_of(share_column(pos, -k, -j, c) * SHARE, SHARE)
    local = pl.multiple_of((((pos[1] - j) % NZ) * 2 + (pos[2] + c) % 2) * SHARE, SHARE)
    return pl.ds(here, SHARE), pl.ds(local, SHARE)


def block_of(pos, k):
    return pl.ds(pl.multiple_of(((pos[0] - k) % NX) * BLOCK, BLOCK), BLOCK)


def mix_kernel(
    pos, sq_ref, more_ref, low_y, high_y, w_ref, p_ref, own, low, high, own_b, low_b, high_b, o_hbm, far_ref, held, sems
):
    square = sq_ref[0:1, 0:1] + more_ref[0:1, 0:1]
    square = square + get_square(low_y)[0:1, 0:1] + get_square(high_y)[0:1, 0:1]
    rate = step_size / jnp.sqrt(square / (HEADS * HD * D) + eps_norm)
    rows = 64
    copies = []
    for n, (k, piece, other) in enumerate(
        ((0, own, own_b), (1, low, low_b), (3, high, high_b), (2, None, None))
    ):

        def step(i, carry, n=n, k=k, piece=piece, other=other):
            start = pl.multiple_of(i * rows, rows)
            here = pl.ds(start, rows)
            for c in range(2):
                for j in range(NZ):
                    at, local = block_columns(pos, k, j, c)
                    weight = w_ref[here, at].astype(F32)
                    stepped = (weight - rate * p_ref[here, at].astype(F32)).astype(BF)
                    value = (mix_share * stepped.astype(F32)).astype(BF)
                    wide = slice(j * SHARE, (j + 1) * SHARE)
                    if piece is None:
                        far_ref[here, local] = value
                    elif c == 0:
                        held[n, here, local] = value + piece[here, wide]
                    else:
                        held[n, here, local] = value + other[here, wide]
            return carry

        lax.fori_loop(0, TOK // rows, step, 0)
        if piece is not None:
            copies.append(
                pltpu.make_async_copy(held.at[n], o_hbm.at[:, block_of(pos, k)], sems.at[n])
            )
            copies[-1].start()
    for copy in copies:
        copy.wait()


def mix(pos, parts, after):
    return kernel_call(
        mix_kernel,
        [array(TOK, D), array(TOK, BLOCK)],
        parts,
        [WHOLE] * 12,
        [pl.BlockSpec(memory_space=pltpu.HBM), WHOLE],
        "mix",
        cost(0, 48 << 20),
        grid=(1,),
        pos=pos,
        scratch=[pltpu.VMEM((3, TOK, BLOCK), BF), pltpu.SemaphoreType.DMA((3,))],
        after=after,
    )


def mix_far_kernel(pos, f_ref, low, high, low_b, high_b, i_hbm, o_hbm, done_ref, held, sem):
    done_ref[...] = jnp.zeros_like(done_ref)
    for rows, pieces in ((FIRST, (low, low_b)), (LAST, (high, high_b))):
        for c, piece in enumerate(pieces):
            for j in range(NZ):
                _, local = block_columns(pos, 2, j, c)
                held[rows, local] = f_ref[rows, local] + piece[:, j * SHARE : (j + 1) * SHARE]
    copy = pltpu.make_async_copy(held, o_hbm.at[:, block_of(pos, 2)], sem)
    copy.start()
    copy.wait()


def mix_far(pos, parts, result):
    return kernel_call(
        mix_far_kernel,
        [array(TOK, D), array(8, 128, dtype=F32)],
        (*parts, result),
        [WHOLE] * 5 + [pl.BlockSpec(memory_space=pltpu.HBM)],
        [pl.BlockSpec(memory_space=pltpu.HBM), WHOLE],
        "mix_far",
        cost(0, 0),
        grid=(1,),
        pos=pos,
        scratch=[pltpu.VMEM((TOK, BLOCK), BF), pltpu.SemaphoreType.DMA],
        alias={6: 0},
    )


def per_device(queries, keys, values_in, out_grad, proj_local, outer_weight, momentum):
    r = lax.axis_index("replica")
    t = lax.axis_index("tensor")
    pos = jnp.stack([r // (NZ * 2), (r // 2) % NZ, r % 2, t // NL, t % NL]).astype(jnp.int32)

    def x_shift(v, d):
        return replica_shift(v, d % NX, 0, 0)

    def z_shift(v, d):
        return replica_shift(v, 0, d % NZ, 0)

    def y_shift(v, d):
        return tensor_shift(v, d % NY, 0)

    def mate_shift(v):
        return tensor_shift(v, 0, 1)

    def core_swap(v):
        return replica_shift(v, 0, 0, 1)

    weight, grad_own = proj_local[0], out_grad
    from_core = core_swap(open_step(pos, weight))
    grad_mate = mate_shift(grad_own)
    own_low, own_high = y_shift(grad_own, 1), y_shift(grad_own, -1)

    x_own, x_up, x_down, x_keep = core_add(pos, weight, from_core, ())
    x_low, x_high = x_shift(x_up, 1), x_shift(x_down, -1)
    context, turned = forward(queries, keys, values_in, (x_up,))
    grad_mate = hold(grad_mate, (context,))
    mate_low, mate_high = y_shift(grad_mate, 1), y_shift(grad_mate, -1)
    send_up, send_down, keep_up, keep_down, kept_own, kept_mate = term(
        pos, context, weight, (grad_mate,)
    )

    x_up2, x_down2 = ring_mid(x_keep, x_low, x_high, (kept_own, own_low, own_high))
    x_low2, x_high2 = x_shift(x_up2, 1), x_shift(x_down2, -1)
    z_own, *to_z = x_add((x_own, x_low, x_high, x_low2, x_high2))
    relay_up, relay_down = relay(
        (own_low, own_high, mate_low, mate_high, send_up, send_down), (z_own,)
    )
    relay_low, relay_high = y_shift(relay_up, 1), y_shift(relay_down, -1)
    from_z = [z_shift(to_z[j - 1], j) for j in (2, 1, 3)]
    new_outer, new_momentum, half = outer_update(
        (z_own, *from_z), outer_weight, momentum, ()
    )

    by_z = {j: z_shift(half, j) for j in (2, 1, 3)}
    pieces = (
        grad_own, grad_mate, own_low, mate_low, own_high, mate_high, relay_low, relay_high
    )
    proj_grad, ctx_grad, square = grads(pos, pieces, weight, turned, (half,))
    square = add_small(square, mate_shift(square), ())
    more = tensor_shift(square, 2, 0)
    group = join_z((half, by_z[1], by_z[2], by_z[3]), (square,))
    g_low, g_high = x_shift(group, 1), x_shift(group, -1)
    send_up2, send_down2 = term_mid((keep_up, keep_down, relay_low, relay_high, square), (group,))
    term_low2, term_high2 = y_shift(send_up2, 1), y_shift(send_down2, -1)
    query_grad, key_grad, value_grad, done = backward(
        queries, keys, values_in, ctx_grad, (send_up2,)
    )
    g_up2, g_down2 = cut(g_low, g_high, (done,))
    g_low2, g_high2 = x_shift(g_up2, 1), x_shift(g_down2, -1)
    near = (group, g_low, g_high)
    send_mate = row_sum(mate_kernel, "mate_sum", kept_mate, term_low2, term_high2, after=(g_up2,))
    term_mate = mate_shift(send_mate)
    new_local, far = mix(
        pos,
        (square, more, term_low2, term_high2, weight, proj_grad, *near, *[core_swap(p) for p in near]),
        (send_mate,),
    )
    new_local, done = mix_far(
        pos, (far, g_low2, g_high2, core_swap(g_low2), core_swap(g_high2)), new_local
    )
    attn_out = row_sum(
        sum_kernel, "attn_sum", kept_own, term_low2, term_high2, term_mate, after=(done,)
    )
    return (attn_out, query_grad, key_grad, value_grad, new_local[None], new_outer, new_momentum)


def solution(mesh):
    return jax.shard_map(
        per_device,
        mesh=mesh,
        in_specs=(
            P("replica", "tensor"),
            P("replica", "tensor"),
            P("replica", "tensor"),
            P(("replica", "tensor"), None),
            P("replica", "tensor", None),
            P("tensor", "replica"),
            P("tensor", "replica"),
        ),
        out_specs=(
            P(("replica", "tensor"), None),
            P("replica", "tensor"),
            P("replica", "tensor"),
            P("replica", "tensor"),
            P("replica", "tensor", None),
            P("tensor", "replica"),
            P("tensor", "replica"),
        ),
        check_vma=False,
    )
```

```python
import functools

import jax
import jax.numpy as jnp
from jax import lax
from jax.experimental import pallas as pl
from jax.experimental.pallas import tpu as pltpu
from jax.sharding import PartitionSpec as P

D = 4096
HEADS = 32
KVH = 8
HD = 128
TOK = 512
ISLANDS = 32
GROUP = HEADS // KVH
NX = 4
NZ = 4
NY = 4
NL = 2
SHARE = 128
ROWS = 64

step_size = 0.02
mu_outer = 0.9
lr_outer = 0.7
mix_share = 0.5
eps_norm = 1e-06
scale_factor = HD ** (-0.5)

WHOLE = pl.BlockSpec(memory_space=pltpu.VMEM)
BF = jnp.bfloat16
F32 = jnp.float32
VMEM_LIMIT = 32 * 1024 * 1024


def params():
    return pltpu.CompilerParams(vmem_limit_bytes=VMEM_LIMIT)


def cost(flops, nbytes, trans=0):
    return pl.CostEstimate(
        flops=int(flops * 0.25), bytes_accessed=int(nbytes * 0.25), transcendentals=int(trans * 0.25)
    )


def kernel_call(kernel, outs, ins, in_specs, out_specs, name, estimate, grid=(), pos=None, scratch=(), after=(), alias=None):
    lead = 0 if pos is None else 1
    skip = len(after)

    def body(*refs):
        kernel(*refs[:lead], *refs[lead + skip :])

    specs = dict(
        grid=grid,
        in_specs=[pl.BlockSpec(memory_space=pl.ANY)] * skip + list(in_specs),
        out_specs=out_specs,
        scratch_shapes=list(scratch),
    )
    if pos is not None:
        specs = dict(grid_spec=pltpu.PrefetchScalarGridSpec(num_scalar_prefetch=1, **specs))
    lead_args = () if pos is None else (pos,)
    return pl.pallas_call(
        body,
        out_shape=outs,
        compiler_params=params(),
        cost_estimate=estimate,
        name=name,
        input_output_aliases=alias or {},
        **specs,
    )(*lead_args, *after, *ins)


def array(*shape, dtype=None):
    return jax.ShapeDtypeStruct(shape, dtype or BF)


def replica_shift(v, dx, dz, dc):
    def at(x, z, c):
        return (x * NZ + z) * 2 + c

    pairs = [
        (at(x, z, c), at((x + dx) % NX, (z + dz) % NZ, (c + dc) % 2))
        for x in range(NX)
        for z in range(NZ)
        for c in range(2)
    ]
    return lax.ppermute(v, "replica", pairs)


def tensor_shift(v, dy, dl):
    pairs = [
        (y * NL + l, ((y + dy) % NY) * NL + (l + dl) % NL) for y in range(NY) for l in range(NL)
    ]
    return lax.ppermute(v, "tensor", pairs)


def tensor_swap(v):
    pairs = [(y * NL + l, (y ^ 1) * NL + l) for y in range(NY) for l in range(NL)]
    return lax.ppermute(v, "tensor", pairs)


def share_column(pos, dx, dz, dc):
    x, z, c = pos[0], pos[1], pos[2]
    return (((x + dx) % NX) * NZ + (z + dz) % NZ) * 2 + (c + dc) % 2


def token_block(pos, dy, dl):
    return ((pos[3] + dy) % NY) * NL + (pos[4] + dl) % NL


FIRST = slice(0, TOK // 2)
LAST = slice(TOK // 2, TOK)


CHUNKS = 8


def open_kernel(pos, w_ref, send_ref):
    for k in range(NX):
        for j in range(NZ):
            at = pl.ds(pl.multiple_of(share_column(pos, k, j, 1) * SHARE, SHARE), SHARE)
            n = (k * NZ + j) * SHARE
            send_ref[:, n : n + SHARE] = w_ref[:, at]


def open_step(pos, weight):
    return kernel_call(
        open_kernel,
        array(TOK, D // 2),
        (weight,),
        [WHOLE],
        WHOLE,
        "open_step",
        cost(0, 8 << 20),
        grid=(1,),
        pos=pos,
    )


def core_add_kernel(pos, w_ref, r_ref, own_ref, up_ref, down_ref, keep_ref):
    for rows, ks in ((FIRST, (0, 2, 3, 1)), (LAST, (0, 1, 2, 3))):
        for ref, k in zip((own_ref, up_ref, down_ref, keep_ref), ks):
            for j in range(NZ):
                at = pl.ds(pl.multiple_of(share_column(pos, k, j, 0) * SHARE, SHARE), SHARE)
                n = (k * NZ + j) * SHARE
                ref[rows, j * SHARE : (j + 1) * SHARE] = (
                    w_ref[rows, at].astype(F32) + r_ref[rows, n : n + SHARE].astype(F32)
                ).astype(BF)


def core_add(pos, weight, got, after):
    return kernel_call(
        core_add_kernel,
        [array(TOK, NZ * SHARE)] * 4,
        (weight, got),
        [WHOLE] * 2,
        [WHOLE] * 4,
        "core_add",
        cost(0, 6 << 20),
        grid=(1,),
        pos=pos,
        after=after,
    )


def ring_mid_kernel(keep_ref, low_ref, high_ref, up_ref, down_ref):
    up_ref[...] = (keep_ref[FIRST, :].astype(F32) + low_ref[FIRST, :].astype(F32)).astype(BF)
    down_ref[...] = (keep_ref[LAST, :].astype(F32) + high_ref[LAST, :].astype(F32)).astype(BF)


def ring_mid(keep, low, high, after=()):
    half = array(TOK // 2, keep.shape[1])
    return kernel_call(
        ring_mid_kernel,
        [half] * 2,
        (keep, low, high),
        [WHOLE] * 3,
        [WHOLE] * 2,
        "ring_mid",
        cost(0, keep.size * 6),
        after=after,
    )


def ring_total(own, low, high, low2, high2, rows, at):
    near, end = (high, low2) if rows == FIRST else (low, high2)
    total = own[rows, at].astype(F32) + near[rows, at].astype(F32)
    return total + end[:, at].astype(F32)


def x_add_kernel(own, low, high, low2, high2, *outs):
    for rows in (FIRST, LAST):
        for j, ref in enumerate(outs):
            at = slice(j * SHARE, (j + 1) * SHARE)
            ref[rows, :] = ring_total(own, low, high, low2, high2, rows, at).astype(BF)


def x_add(parts, after=()):
    return kernel_call(
        x_add_kernel,
        [array(TOK, SHARE)] * 4,
        parts,
        [WHOLE] * 5,
        [WHOLE] * 4,
        "x_add",
        cost(0, 5 << 19),
        after=after,
    )


def outer_kernel(own, one, two, three, ow_ref, mo_ref, no_ref, nm_ref, nb_ref):
    total = own[...].astype(F32) + one[...].astype(F32)
    total = total + two[...].astype(F32)
    total = total + three[...].astype(F32)
    outer = ow_ref[...]
    delta = outer - total / ISLANDS
    moment = mu_outer * mo_ref[...] + delta
    new = outer - lr_outer * (mu_outer * moment + delta)
    no_ref[...] = new
    nm_ref[...] = moment
    nb_ref[...] = ((1.0 - mix_share) * new.astype(BF).astype(F32)).astype(BF)


def outer_update(parts, outer_weight, momentum, after):
    f32 = array(TOK, SHARE, dtype=F32)
    return kernel_call(
        outer_kernel,
        [f32, f32, array(TOK, SHARE)],
        (*parts, outer_weight, momentum),
        [WHOLE] * 6,
        [WHOLE] * 3,
        "outer_update",
        cost(0, 2 << 20),
        after=after,
    )


def cut_kernel(low_ref, high_ref, up_ref, down_ref):
    up_ref[...] = low_ref[FIRST, :]
    down_ref[...] = high_ref[LAST, :]


def cut(low, high, after=()):
    return kernel_call(
        cut_kernel,
        [array(TOK // 2, low.shape[1])] * 2,
        (low, high),
        [WHOLE] * 2,
        [WHOLE] * 2,
        "cut",
        cost(0, low.size * 4),
        after=after,
    )


def join_z_kernel(*refs):
    for j, ref in enumerate(refs[:-1]):
        refs[-1][:, j * SHARE : (j + 1) * SHARE] = ref[...]


def join_z(parts, after=()):
    return kernel_call(
        join_z_kernel,
        array(TOK, NZ * SHARE),
        parts,
        [WHOLE] * NZ,
        WHOLE,
        "join_z",
        cost(1e11, 1 << 20),
        after=after,
    )


def stack_kernel(*refs):
    start = 0
    for ref in refs[:-1]:
        rows = ref.shape[0]
        refs[-1][start : start + rows, :] = ref[...]
        start += rows


def stack(parts, after=()):
    rows, columns = sum(p.shape[0] for p in parts), parts[0].shape[1]
    return kernel_call(
        stack_kernel,
        array(rows, columns),
        parts,
        [WHOLE] * len(parts),
        WHOLE,
        "stack",
        cost(0, rows * columns * 4),
        after=after,
    )


def hold_kernel(a_ref, o_ref):
    o_ref[...] = a_ref[...]


def hold(a, after):
    return kernel_call(
        hold_kernel,
        array(*a.shape),
        (a,),
        [WHOLE],
        WHOLE,
        "hold",
        cost(0, a.size * 4),
        after=after,
    )


POWER = scale_factor * 1.4426950408889634


def dot(a, b, ca, cb):
    return lax.dot_general(a, b, (((ca,), (cb,)), ((), ())), preferred_element_type=F32)


def probs_of(q, k):
    scores = dot(k, q, 1, 1)
    shape = scores.shape
    causal = lax.broadcasted_iota(jnp.int32, shape, 0) <= lax.broadcasted_iota(jnp.int32, shape, 1)
    scores = jnp.where(causal, scores, -jnp.inf)
    highest = jnp.max(scores, axis=0, keepdims=True)
    expon = jnp.exp2(scores * POWER - highest * POWER)
    return expon * (1.0 / jnp.sum(expon, axis=0, keepdims=True))


def forward_kernel(q_ref, k_ref, v_ref, o_ref, t_ref):
    turned = v_ref[...].T
    for h in range(GROUP):
        head = slice(h * HD, (h + 1) * HD)
        probs = probs_of(q_ref[:, head], k_ref[...]).astype(BF)
        out = dot(turned, probs, 1, 0).astype(BF)
        t_ref[head, :] = out
        o_ref[:, head] = out.T


def forward(queries, keys, values, after):
    return kernel_call(
        forward_kernel,
        [array(TOK, GROUP * HD), array(GROUP * HD, TOK)],
        (queries, keys, values),
        [WHOLE] * 3,
        [WHOLE] * 2,
        "forward",
        cost(5e8, 2 << 20, 1 << 20),
        after=after,
    )


def backward_kernel(q_ref, k_ref, v_ref, g_ref, dq_ref, dk_ref, dv_ref, done_ref):
    done_ref[...] = jnp.zeros_like(done_ref)
    key_grad = jnp.zeros((TOK, HD), F32)
    value_grad = jnp.zeros((TOK, HD), F32)
    k, v = k_ref[...], v_ref[...]
    for h in range(GROUP):
        head = slice(h * HD, (h + 1) * HD)
        q, g = q_ref[:, head], g_ref[:, head]
        probs = probs_of(q, k)
        prob_grad = dot(v, g, 1, 1)
        inner = jnp.sum(prob_grad * probs, axis=0, keepdims=True)
        score_grad = (probs * (prob_grad - inner) * scale_factor).astype(BF)
        dq_ref[:, head] = dot(score_grad, k, 0, 0).astype(BF)
        key_grad += dot(score_grad, q, 1, 0)
        value_grad += dot(probs.astype(BF), g, 1, 0)
    dk_ref[...] = key_grad.astype(BF)
    dv_ref[...] = value_grad.astype(BF)


def backward(queries, keys, values, ctx_grad, after):
    return kernel_call(
        backward_kernel,
        [array(TOK, GROUP * HD), array(TOK, HD), array(TOK, HD), array(8, 128, dtype=F32)],
        (queries, keys, values, ctx_grad),
        [WHOLE] * 4,
        [WHOLE] * 4,
        "backward",
        cost(1.3e9, 3 << 20, 1 << 20),
        after=after,
    )


TILE = 512


HALF_ROWS = ROWS // 2


def term_kernel(
    pos, c_ref, w_ref, up_ref, down_ref, keep_up_ref, keep_down_ref, own_ref, mate_ref, held
):
    at = pl.ds(pl.multiple_of(pl.program_id(0) * TILE, TILE), TILE)
    held[...] = dot(c_ref[...], w_ref[:, at], 1, 0).astype(BF)

    def rows(dy, dl, first=0, count=ROWS):
        row = pl.multiple_of(token_block(pos, dy, dl) * ROWS + first, HALF_ROWS)
        return held[pl.ds(row, count), :]

    for dl in range(NL):
        low = slice(dl * HALF_ROWS, (dl + 1) * HALF_ROWS)
        up_ref[low, at] = rows(2, dl, 0, HALF_ROWS)
        down_ref[low, at] = rows(2, dl, HALF_ROWS, HALF_ROWS)
        full = slice(dl * ROWS, (dl + 1) * ROWS)
        keep_up_ref[full, at] = rows(1, dl)
        keep_down_ref[full, at] = rows(3, dl)
    own_ref[:, at] = rows(0, 0)
    mate_ref[:, at] = rows(0, 1)


def term(pos, context, weight, after):
    return kernel_call(
        term_kernel,
        [array(ROWS, D)] * 2 + [array(2 * ROWS, D)] * 2 + [array(ROWS, D)] * 2,
        (context, weight),
        [WHOLE, WHOLE],
        [WHOLE] * 6,
        "term",
        cost(2.1e9, 9 << 20),
        grid=(D // TILE,),
        pos=pos,
        scratch=[pltpu.VMEM((TOK, TILE), BF)],
        after=after,
    )


PAD = 128
WIDE = D + PAD


def get_square(ref):
    return ref[0:16, D:WIDE].astype(F32) + ref[16:32, D:WIDE].astype(F32)


def term_mid_kernel(keep_up_ref, keep_down_ref, low_ref, high_ref, sq_ref, up_ref, down_ref):
    square = jnp.concatenate([sq_ref[...]] * 2, axis=0)
    high = square.astype(BF)
    for ref in (up_ref, down_ref):
        ref[:, D:WIDE] = jnp.zeros((2 * ROWS, PAD), BF)
        ref[0:16, D:WIDE] = high
        ref[16:32, D:WIDE] = (square - high.astype(F32)).astype(BF)
    for dl in range(NL):
        part = slice(ROWS + dl * HALF_ROWS, ROWS + (dl + 1) * HALF_ROWS)
        first = slice(dl * ROWS, dl * ROWS + HALF_ROWS)
        last = slice(dl * ROWS + HALF_ROWS, (dl + 1) * ROWS)
        up_ref[first, 0:D] = (
            keep_up_ref[first, :].astype(F32) + low_ref[part, :].astype(F32)
        ).astype(BF)
        up_ref[last, 0:D] = keep_up_ref[last, :]
        down_ref[first, 0:D] = keep_down_ref[first, :]
        down_ref[last, 0:D] = (
            keep_down_ref[last, :].astype(F32) + high_ref[part, :].astype(F32)
        ).astype(BF)


def term_mid(parts, after):
    return kernel_call(
        term_mid_kernel,
        [array(2 * ROWS, WIDE)] * 2,
        parts,
        [WHOLE] * 5,
        [WHOLE] * 2,
        "term_mid",
        cost(0, 5 << 20),
        after=after,
    )


def sum_kernel(own_ref, up_ref, down_ref, mate_ref, o_ref):
    total = own_ref[...].astype(F32) + up_ref[0:ROWS, 0:D].astype(F32)
    total = total + down_ref[0:ROWS, 0:D].astype(F32)
    o_ref[...] = (total + mate_ref[...].astype(F32)).astype(BF)


def mate_kernel(mate_ref, up_ref, down_ref, o_ref):
    total = mate_ref[...].astype(F32) + up_ref[ROWS : 2 * ROWS, 0:D].astype(F32)
    o_ref[...] = (total + down_ref[ROWS : 2 * ROWS, 0:D].astype(F32)).astype(BF)


def square_kernel(sq_ref, more_ref, up_ref, down_ref, o_ref):
    square = sq_ref[...] + more_ref[...]
    o_ref[...] = square + get_square(up_ref)[0:8] + get_square(down_ref)[0:8]


def square_sum(parts, after):
    return kernel_call(
        square_kernel,
        array(8, 128, dtype=F32),
        parts,
        [WHOLE] * 4,
        WHOLE,
        "square_sum",
        cost(0, 1 << 16),
        after=after,
    )


def row_sum(kernel, name, *parts, after=(), flops=0):
    return kernel_call(
        kernel,
        array(ROWS, D),
        parts,
        [WHOLE] * len(parts),
        WHOLE,
        name,
        cost(flops, ROWS * D * 2 * (len(parts) + 1)),
        after=after,
    )


def relay_kernel(
    own_low, own_high, mate_low, mate_high, term_up, term_down, up_ref, down_ref
):
    for n, (low, high) in enumerate(((own_low, own_high), (mate_low, mate_high))):
        part = slice(n * HALF_ROWS, (n + 1) * HALF_ROWS)
        up_ref[part, :] = low[0:HALF_ROWS, :]
        down_ref[part, :] = high[HALF_ROWS:ROWS, :]
    up_ref[ROWS : 2 * ROWS, :] = term_up[...]
    down_ref[ROWS : 2 * ROWS, :] = term_down[...]


def relay(parts, after):
    return kernel_call(
        relay_kernel,
        [array(2 * ROWS, D)] * 2,
        parts,
        [WHOLE] * 6,
        [WHOLE] * 2,
        "relay",
        cost(0, 4 << 20),
        after=after,
    )


def add_kernel(a_ref, b_ref, o_ref):
    o_ref[...] = a_ref[...] + b_ref[...]


def add_small(a, b, after):
    return kernel_call(
        add_kernel,
        array(8, 128, dtype=F32),
        (a, b),
        [WHOLE] * 2,
        WHOLE,
        "add_small",
        cost(0, 1 << 14),
        after=after,
    )


def grads_kernel(pos, *refs):
    pieces, (w_ref, t_ref, proj_ref, ctx_ref, sq_ref, held) = refs[:8], refs[8:]

    def place(dy, dl, piece, first=0):
        row = pl.multiple_of(token_block(pos, dy, dl) * ROWS + first, HALF_ROWS)
        held[pl.ds(row, piece.shape[0]), :] = piece

    for n, (dy, dl) in enumerate(((0, 0), (0, 1), (-1, 0), (-1, 1), (1, 0), (1, 1))):
        place(dy, dl, pieces[n][...])
    for dl in range(NL):
        part = slice(dl * HALF_ROWS, (dl + 1) * HALF_ROWS)
        place(2, dl, pieces[6][part, :])
        place(2, dl, pieces[7][part, :], HALF_ROWS)

    ctx_ref[...] = dot(held[...], w_ref[...], 1, 1).astype(BF)
    turned = t_ref[...]
    square = jnp.zeros((8, TILE), F32)
    for i in range(D // TILE):
        at = slice(i * TILE, (i + 1) * TILE)
        proj = dot(turned, held[:, at], 1, 0)
        proj_ref[:, at] = proj.astype(BF)
        square += jnp.sum((proj * proj).reshape(TOK // 8, 8, TILE), axis=0)
    sq_ref[...] = jnp.broadcast_to(jnp.sum(square, axis=(0, 1), keepdims=True), (8, 128))


def grads(pos, pieces, weight, turned, after):
    hq = GROUP * HD
    return kernel_call(
        grads_kernel,
        [array(hq, D), array(TOK, hq), array(8, 128, dtype=F32)],
        (*pieces, weight, turned),
        [WHOLE] * 10,
        [WHOLE] * 3,
        "grads",
        cost(4.3e9, 13 << 20),
        grid=(1,),
        pos=pos,
        scratch=[pltpu.VMEM((TOK, D), BF)],
        after=after,
    )


BLOCK = D // NX


def block_columns(pos, k, j, c):
    here = pl.multiple_of(share_column(pos, -k, -j, c) * SHARE, SHARE)
    local = pl.multiple_of((((pos[1] - j) % NZ) * 2 + (pos[2] + c) % 2) * SHARE, SHARE)
    return pl.ds(here, SHARE), pl.ds(local, SHARE)


def block_of(pos, k):
    return pl.ds(pl.multiple_of(((pos[0] - k) % NX) * BLOCK, BLOCK), BLOCK)


def mix_kernel(pos, sq_ref, more_ref, w_ref, p_ref, own, low, low2, high2, high, o_ref):
    square = sq_ref[0:1, 0:1] + more_ref[0:1, 0:1]
    rate = step_size / jnp.sqrt(square / (HEADS * HD * D) + eps_norm)
    rows = 32

    def step(i, carry):
        here = pl.ds(pl.multiple_of(i * rows, rows), rows)
        late = i >= TOK // 2 // rows
        there = pl.ds(pl.multiple_of((i % (TOK // 2 // rows)) * rows, rows), rows)
        for k, piece in enumerate((own, low, None, high)):
            for c in range(2):
                for j in range(NZ):
                    at, _ = block_columns(pos, k, j, c)
                    weight = w_ref[here, at].astype(F32)
                    stepped = (weight - rate * p_ref[here, at].astype(F32)).astype(BF)
                    value = (mix_share * stepped.astype(F32)).astype(BF)
                    wide = slice(j * SHARE, (j + 1) * SHARE)
                    if c == 0 and piece is not None:
                        value = value + piece[here, wide]
                    elif c == 0:
                        value = value + jnp.where(late, high2[there, wide], low2[there, wide])
                    o_ref[here, at] = value
        return carry

    lax.fori_loop(0, TOK // rows, step, 0)


def mix(pos, parts, after):
    return kernel_call(
        mix_kernel,
        array(TOK, D),
        parts,
        [WHOLE] * 9,
        WHOLE,
        "mix",
        cost(0, 48 << 20),
        grid=(1,),
        pos=pos,
        after=after,
    )


def mix_other_kernel(pos, part_ref, got_ref, o_hbm, done_ref, held, sems):
    done_ref[...] = jnp.zeros_like(done_ref)
    rows = TOK // CHUNKS
    copies = []
    for i in range(CHUNKS):
        here = slice(i * rows, (i + 1) * rows)
        for k in range(NX):
            there = slice(k * TOK + i * rows, k * TOK + (i + 1) * rows)
            for j in range(NZ):
                at, _ = block_columns(pos, k, j, 0)
                held[here, at] = part_ref[here, at]
                at, _ = block_columns(pos, k, j, 1)
                held[here, at] = part_ref[here, at] + got_ref[there, j * SHARE : (j + 1) * SHARE]
        copies.append(pltpu.make_async_copy(held.at[here], o_hbm.at[here], sems.at[i]))
        copies[-1].start()
    for copy in copies:
        copy.wait()


def mix_other(pos, part, got):
    return kernel_call(
        mix_other_kernel,
        [array(TOK, D), array(8, 128, dtype=F32)],
        (part, got),
        [WHOLE] * 2,
        [pl.BlockSpec(memory_space=pltpu.HBM), WHOLE],
        "mix_other",
        cost(0, 0),
        grid=(1,),
        pos=pos,
        scratch=[pltpu.VMEM((TOK, D), BF), pltpu.SemaphoreType.DMA((CHUNKS,))],
    )


def per_device(queries, keys, values_in, out_grad, proj_local, outer_weight, momentum):
    r = lax.axis_index("replica")
    t = lax.axis_index("tensor")
    pos = jnp.stack([r // (NZ * 2), (r // 2) % NZ, r % 2, t // NL, t % NL]).astype(jnp.int32)

    def x_shift(v, d):
        return replica_shift(v, d % NX, 0, 0)

    def z_shift(v, d):
        return replica_shift(v, 0, d % NZ, 0)

    def y_shift(v, d):
        return tensor_shift(v, d % NY, 0)

    def mate_shift(v):
        return tensor_shift(v, 0, 1)

    def core_swap(v):
        return replica_shift(v, 0, 0, 1)

    weight, grad_own = proj_local[0], out_grad
    from_core = core_swap(open_step(pos, weight))
    grad_mate = mate_shift(grad_own)
    own_low, own_high = y_shift(grad_own, 1), y_shift(grad_own, -1)

    x_own, x_up, x_down, x_keep = core_add(pos, weight, from_core, ())
    x_low, x_high = x_shift(x_up, 1), x_shift(x_down, -1)
    context, turned = forward(queries, keys, values_in, (x_up,))
    grad_mate = hold(grad_mate, (context,))
    mate_low, mate_high = y_shift(grad_mate, 1), y_shift(grad_mate, -1)
    send_up, send_down, keep_up, keep_down, kept_own, kept_mate = term(
        pos, context, weight, (grad_mate,)
    )

    x_up2, x_down2 = ring_mid(x_keep, x_low, x_high, (kept_own, own_low, own_high))
    x_low2, x_high2 = x_shift(x_up2, 1), x_shift(x_down2, -1)
    z_own, *to_z = x_add((x_own, x_low, x_high, x_low2, x_high2))
    relay_up, relay_down = relay(
        (own_low, own_high, mate_low, mate_high, send_up, send_down), (z_own,)
    )
    relay_low, relay_high = y_shift(relay_up, 1), y_shift(relay_down, -1)
    from_z = [z_shift(to_z[j - 1], j) for j in (2, 1, 3)]
    new_outer, new_momentum, half = outer_update(
        (z_own, *from_z), outer_weight, momentum, ()
    )

    by_z = {j: z_shift(half, j) for j in (2, 1, 3)}
    pieces = (
        grad_own, grad_mate, own_low, mate_low, own_high, mate_high, relay_low, relay_high
    )
    proj_grad, ctx_grad, square = grads(pos, pieces, weight, turned, (half,))
    more = tensor_shift(square, 2, 0)
    send_up2, send_down2 = term_mid((keep_up, keep_down, relay_low, relay_high, square), (square,))
    term_low2, term_high2 = y_shift(send_up2, 1), y_shift(send_down2, -1)
    group = join_z((half, by_z[1], by_z[2], by_z[3]), (send_up2,))
    g_low, g_high = x_shift(group, 1), x_shift(group, -1)
    query_grad, key_grad, value_grad, done = backward(
        queries, keys, values_in, ctx_grad, (group,)
    )
    g_up2, g_down2 = cut(g_low, g_high, (done,))
    g_low2, g_high2 = x_shift(g_up2, 1), x_shift(g_down2, -1)
    square = square_sum((square, more, term_low2, term_high2), (g_up2,))
    more = mate_shift(square)
    send_mate = row_sum(mate_kernel, "mate_sum", kept_mate, term_low2, term_high2, after=(more,))
    term_mate = mate_shift(send_mate)
    rest = stack((group, g_low, g_low2, g_high2, g_high), (send_mate,))
    part = mix(
        pos,
        (square, more, weight, proj_grad, group, g_low, g_low2, g_high2, g_high),
        (rest,),
    )
    new_local, done = mix_other(pos, part, core_swap(rest))
    attn_out = row_sum(
        sum_kernel, "attn_sum", kept_own, term_low2, term_high2, term_mate, after=(done,)
    )
    return (attn_out, query_grad, key_grad, value_grad, new_local[None], new_outer, new_momentum)


def solution(mesh):
    return jax.shard_map(
        per_device,
        mesh=mesh,
        in_specs=(
            P("replica", "tensor"),
            P("replica", "tensor"),
            P("replica", "tensor"),
            P(("replica", "tensor"), None),
            P("replica", "tensor", None),
            P("tensor", "replica"),
            P("tensor", "replica"),
        ),
        out_specs=(
            P(("replica", "tensor"), None),
            P("replica", "tensor"),
            P("replica", "tensor"),
            P("replica", "tensor"),
            P("replica", "tensor", None),
            P("tensor", "replica"),
            P("tensor", "replica"),
        ),
        check_vma=False,
    )
```

```python
import functools

import jax
import jax.numpy as jnp
from jax import lax
from jax.experimental import pallas as pl
from jax.experimental.pallas import tpu as pltpu
from jax.sharding import PartitionSpec as P

D = 4096
HEADS = 32
KVH = 8
HD = 128
TOK = 512
ISLANDS = 32
GROUP = HEADS // KVH
NX = 4
NZ = 4
NY = 4
NL = 2
SHARE = 128
ROWS = 64

step_size = 0.02
mu_outer = 0.9
lr_outer = 0.7
mix_share = 0.5
eps_norm = 1e-06
scale_factor = HD ** (-0.5)

WHOLE = pl.BlockSpec(memory_space=pltpu.VMEM)
BF = jnp.bfloat16
F32 = jnp.float32
VMEM_LIMIT = 32 * 1024 * 1024


def params():
    return pltpu.CompilerParams(vmem_limit_bytes=VMEM_LIMIT)


def cost(flops, nbytes, trans=0):
    return pl.CostEstimate(
        flops=int(flops * 0.25), bytes_accessed=int(nbytes * 0.25), transcendentals=int(trans * 0.25)
    )


def kernel_call(kernel, outs, ins, in_specs, out_specs, name, estimate, grid=(), pos=None, scratch=(), after=(), alias=None):
    lead = 0 if pos is None else 1
    skip = len(after)

    def body(*refs):
        kernel(*refs[:lead], *refs[lead + skip :])

    specs = dict(
        grid=grid,
        in_specs=[pl.BlockSpec(memory_space=pl.ANY)] * skip + list(in_specs),
        out_specs=out_specs,
        scratch_shapes=list(scratch),
    )
    if pos is not None:
        specs = dict(grid_spec=pltpu.PrefetchScalarGridSpec(num_scalar_prefetch=1, **specs))
    lead_args = () if pos is None else (pos,)
    return pl.pallas_call(
        body,
        out_shape=outs,
        compiler_params=params(),
        cost_estimate=estimate,
        name=name,
        input_output_aliases=alias or {},
        **specs,
    )(*lead_args, *after, *ins)


def array(*shape, dtype=None):
    return jax.ShapeDtypeStruct(shape, dtype or BF)


def replica_shift(v, dx, dz, dc):
    def at(x, z, c):
        return (x * NZ + z) * 2 + c

    pairs = [
        (at(x, z, c), at((x + dx) % NX, (z + dz) % NZ, (c + dc) % 2))
        for x in range(NX)
        for z in range(NZ)
        for c in range(2)
    ]
    return lax.ppermute(v, "replica", pairs)


def tensor_shift(v, dy, dl):
    pairs = [
        (y * NL + l, ((y + dy) % NY) * NL + (l + dl) % NL) for y in range(NY) for l in range(NL)
    ]
    return lax.ppermute(v, "tensor", pairs)


def tensor_swap(v):
    pairs = [(y * NL + l, (y ^ 1) * NL + l) for y in range(NY) for l in range(NL)]
    return lax.ppermute(v, "tensor", pairs)


def share_column(pos, dx, dz, dc):
    x, z, c = pos[0], pos[1], pos[2]
    return (((x + dx) % NX) * NZ + (z + dz) % NZ) * 2 + (c + dc) % 2


def token_block(pos, dy, dl):
    return ((pos[3] + dy) % NY) * NL + (pos[4] + dl) % NL


FIRST = slice(0, TOK // 2)
LAST = slice(TOK // 2, TOK)


CHUNKS = 8


def open_kernel(pos, w_ref, send_ref):
    for k in range(NX):
        for j in range(NZ):
            at = pl.ds(pl.multiple_of(share_column(pos, k, j, 1) * SHARE, SHARE), SHARE)
            n = (k * NZ + j) * SHARE
            send_ref[:, n : n + SHARE] = w_ref[:, at]


def open_step(pos, weight):
    return kernel_call(
        open_kernel,
        array(TOK, D // 2),
        (weight,),
        [WHOLE],
        WHOLE,
        "open_step",
        cost(0, 8 << 20),
        grid=(1,),
        pos=pos,
    )


def core_add_kernel(pos, w_ref, r_ref, own_ref, up_ref, down_ref, keep_ref):
    for rows, ks in ((FIRST, (0, 2, 3, 1)), (LAST, (0, 1, 2, 3))):
        for ref, k in zip((own_ref, up_ref, down_ref, keep_ref), ks):
            for j in range(NZ):
                at = pl.ds(pl.multiple_of(share_column(pos, k, j, 0) * SHARE, SHARE), SHARE)
                n = (k * NZ + j) * SHARE
                ref[rows, j * SHARE : (j + 1) * SHARE] = (
                    w_ref[rows, at].astype(F32) + r_ref[rows, n : n + SHARE].astype(F32)
                ).astype(BF)


def core_add(pos, weight, got, after):
    return kernel_call(
        core_add_kernel,
        [array(TOK, NZ * SHARE)] * 4,
        (weight, got),
        [WHOLE] * 2,
        [WHOLE] * 4,
        "core_add",
        cost(0, 6 << 20),
        grid=(1,),
        pos=pos,
        after=after,
    )


def ring_mid_kernel(keep_ref, low_ref, high_ref, up_ref, down_ref):
    up_ref[...] = (keep_ref[FIRST, :].astype(F32) + low_ref[FIRST, :].astype(F32)).astype(BF)
    down_ref[...] = (keep_ref[LAST, :].astype(F32) + high_ref[LAST, :].astype(F32)).astype(BF)


def ring_mid(keep, low, high, after=()):
    half = array(TOK // 2, keep.shape[1])
    return kernel_call(
        ring_mid_kernel,
        [half] * 2,
        (keep, low, high),
        [WHOLE] * 3,
        [WHOLE] * 2,
        "ring_mid",
        cost(0, keep.size * 6),
        after=after,
    )


def ring_total(own, low, high, low2, high2, rows, at):
    near, end = (high, low2) if rows == FIRST else (low, high2)
    total = own[rows, at].astype(F32) + near[rows, at].astype(F32)
    return total + end[:, at].astype(F32)


def x_add_kernel(own, low, high, low2, high2, *outs):
    for rows in (FIRST, LAST):
        for j, ref in enumerate(outs):
            at = slice(j * SHARE, (j + 1) * SHARE)
            ref[rows, :] = ring_total(own, low, high, low2, high2, rows, at).astype(BF)


def x_add(parts, after=()):
    return kernel_call(
        x_add_kernel,
        [array(TOK, SHARE)] * 4,
        parts,
        [WHOLE] * 5,
        [WHOLE] * 4,
        "x_add",
        cost(0, 5 << 19),
        after=after,
    )


def outer_kernel(own, one, two, three, ow_ref, mo_ref, no_ref, nm_ref, nb_ref):
    total = own[...].astype(F32) + one[...].astype(F32)
    total = total + two[...].astype(F32)
    total = total + three[...].astype(F32)
    outer = ow_ref[...]
    delta = outer - total / ISLANDS
    moment = mu_outer * mo_ref[...] + delta
    new = outer - lr_outer * (mu_outer * moment + delta)
    no_ref[...] = new
    nm_ref[...] = moment
    nb_ref[...] = ((1.0 - mix_share) * new.astype(BF).astype(F32)).astype(BF)


def outer_update(parts, outer_weight, momentum, after):
    f32 = array(TOK, SHARE, dtype=F32)
    return kernel_call(
        outer_kernel,
        [f32, f32, array(TOK, SHARE)],
        (*parts, outer_weight, momentum),
        [WHOLE] * 6,
        [WHOLE] * 3,
        "outer_update",
        cost(0, 2 << 20),
        after=after,
    )


def cut_kernel(low_ref, high_ref, up_ref, down_ref):
    up_ref[...] = low_ref[FIRST, :]
    down_ref[...] = high_ref[LAST, :]


def cut(low, high, after=()):
    return kernel_call(
        cut_kernel,
        [array(TOK // 2, low.shape[1])] * 2,
        (low, high),
        [WHOLE] * 2,
        [WHOLE] * 2,
        "cut",
        cost(0, low.size * 4),
        after=after,
    )


def join_z_kernel(*refs):
    for j, ref in enumerate(refs[:-1]):
        refs[-1][:, j * SHARE : (j + 1) * SHARE] = ref[...]


def join_z(parts, after=()):
    return kernel_call(
        join_z_kernel,
        array(TOK, NZ * SHARE),
        parts,
        [WHOLE] * NZ,
        WHOLE,
        "join_z",
        cost(1e11, 1 << 20),
        after=after,
    )


def hold_kernel(a_ref, o_ref):
    o_ref[...] = a_ref[...]


def hold(a, after):
    return kernel_call(
        hold_kernel,
        array(*a.shape),
        (a,),
        [WHOLE],
        WHOLE,
        "hold",
        cost(0, a.size * 4),
        after=after,
    )


POWER = scale_factor * 1.4426950408889634


def dot(a, b, ca, cb):
    return lax.dot_general(a, b, (((ca,), (cb,)), ((), ())), preferred_element_type=F32)


def probs_of(q, k):
    scores = dot(k, q, 1, 1)
    shape = scores.shape
    causal = lax.broadcasted_iota(jnp.int32, shape, 0) <= lax.broadcasted_iota(jnp.int32, shape, 1)
    scores = jnp.where(causal, scores, -jnp.inf)
    highest = jnp.max(scores, axis=0, keepdims=True)
    expon = jnp.exp2(scores * POWER - highest * POWER)
    return expon * (1.0 / jnp.sum(expon, axis=0, keepdims=True))


def forward_kernel(q_ref, k_ref, v_ref, o_ref, t_ref):
    turned = v_ref[...].T
    for h in range(GROUP):
        head = slice(h * HD, (h + 1) * HD)
        probs = probs_of(q_ref[:, head], k_ref[...]).astype(BF)
        out = dot(turned, probs, 1, 0).astype(BF)
        t_ref[head, :] = out
        o_ref[:, head] = out.T


def forward(queries, keys, values, after):
    return kernel_call(
        forward_kernel,
        [array(TOK, GROUP * HD), array(GROUP * HD, TOK)],
        (queries, keys, values),
        [WHOLE] * 3,
        [WHOLE] * 2,
        "forward",
        cost(5e8, 2 << 20, 1 << 20),
        after=after,
    )


def backward_kernel(q_ref, k_ref, v_ref, g_ref, dq_ref, dk_ref, dv_ref, done_ref):
    done_ref[...] = jnp.zeros_like(done_ref)
    key_grad = jnp.zeros((TOK, HD), F32)
    value_grad = jnp.zeros((TOK, HD), F32)
    k, v = k_ref[...], v_ref[...]
    for h in range(GROUP):
        head = slice(h * HD, (h + 1) * HD)
        q, g = q_ref[:, head], g_ref[:, head]
        probs = probs_of(q, k)
        prob_grad = dot(v, g, 1, 1)
        inner = jnp.sum(prob_grad * probs, axis=0, keepdims=True)
        score_grad = (probs * (prob_grad - inner) * scale_factor).astype(BF)
        dq_ref[:, head] = dot(score_grad, k, 0, 0).astype(BF)
        key_grad += dot(score_grad, q, 1, 0)
        value_grad += dot(probs.astype(BF), g, 1, 0)
    dk_ref[...] = key_grad.astype(BF)
    dv_ref[...] = value_grad.astype(BF)


def backward(queries, keys, values, ctx_grad, after):
    return kernel_call(
        backward_kernel,
        [array(TOK, GROUP * HD), array(TOK, HD), array(TOK, HD), array(8, 128, dtype=F32)],
        (queries, keys, values, ctx_grad),
        [WHOLE] * 4,
        [WHOLE] * 4,
        "backward",
        cost(1.3e9, 3 << 20, 1 << 20),
        after=after,
    )


TILE = 512


HALF_ROWS = ROWS // 2


def term_kernel(
    pos, c_ref, w_ref, up_ref, down_ref, keep_up_ref, keep_down_ref, own_ref, mate_ref, held
):
    at = pl.ds(pl.multiple_of(pl.program_id(0) * TILE, TILE), TILE)
    held[...] = dot(c_ref[...], w_ref[:, at], 1, 0).astype(BF)

    def rows(dy, dl, first=0, count=ROWS):
        row = pl.multiple_of(token_block(pos, dy, dl) * ROWS + first, HALF_ROWS)
        return held[pl.ds(row, count), :]

    for dl in range(NL):
        low = slice(dl * HALF_ROWS, (dl + 1) * HALF_ROWS)
        up_ref[low, at] = rows(2, dl, 0, HALF_ROWS)
        down_ref[low, at] = rows(2, dl, HALF_ROWS, HALF_ROWS)
        full = slice(dl * ROWS, (dl + 1) * ROWS)
        keep_up_ref[full, at] = rows(1, dl)
        keep_down_ref[full, at] = rows(3, dl)
    own_ref[:, at] = rows(0, 0)
    mate_ref[:, at] = rows(0, 1)


def term(pos, context, weight, after):
    return kernel_call(
        term_kernel,
        [array(ROWS, D)] * 2 + [array(2 * ROWS, D)] * 2 + [array(ROWS, D)] * 2,
        (context, weight),
        [WHOLE, WHOLE],
        [WHOLE] * 6,
        "term",
        cost(2.1e9, 9 << 20),
        grid=(D // TILE,),
        pos=pos,
        scratch=[pltpu.VMEM((TOK, TILE), BF)],
        after=after,
    )


PAD = 128
WIDE = D + PAD


def get_square(ref):
    return ref[0:16, D:WIDE].astype(F32) + ref[16:32, D:WIDE].astype(F32)


def term_mid_kernel(keep_up_ref, keep_down_ref, low_ref, high_ref, sq_ref, up_ref, down_ref):
    square = jnp.concatenate([sq_ref[...]] * 2, axis=0)
    high = square.astype(BF)
    for ref in (up_ref, down_ref):
        ref[:, D:WIDE] = jnp.zeros((2 * ROWS, PAD), BF)
        ref[0:16, D:WIDE] = high
        ref[16:32, D:WIDE] = (square - high.astype(F32)).astype(BF)
    for dl in range(NL):
        part = slice(ROWS + dl * HALF_ROWS, ROWS + (dl + 1) * HALF_ROWS)
        first = slice(dl * ROWS, dl * ROWS + HALF_ROWS)
        last = slice(dl * ROWS + HALF_ROWS, (dl + 1) * ROWS)
        up_ref[first, 0:D] = (
            keep_up_ref[first, :].astype(F32) + low_ref[part, :].astype(F32)
        ).astype(BF)
        up_ref[last, 0:D] = keep_up_ref[last, :]
        down_ref[first, 0:D] = keep_down_ref[first, :]
        down_ref[last, 0:D] = (
            keep_down_ref[last, :].astype(F32) + high_ref[part, :].astype(F32)
        ).astype(BF)


def term_mid(parts, after):
    return kernel_call(
        term_mid_kernel,
        [array(2 * ROWS, WIDE)] * 2,
        parts,
        [WHOLE] * 5,
        [WHOLE] * 2,
        "term_mid",
        cost(0, 5 << 20),
        after=after,
    )


def sum_kernel(own_ref, up_ref, down_ref, mate_ref, o_ref):
    total = own_ref[...].astype(F32) + up_ref[0:ROWS, 0:D].astype(F32)
    total = total + down_ref[0:ROWS, 0:D].astype(F32)
    o_ref[...] = (total + mate_ref[...].astype(F32)).astype(BF)


def mate_kernel(mate_ref, up_ref, down_ref, o_ref):
    total = mate_ref[...].astype(F32) + up_ref[ROWS : 2 * ROWS, 0:D].astype(F32)
    o_ref[...] = (total + down_ref[ROWS : 2 * ROWS, 0:D].astype(F32)).astype(BF)


def square_kernel(sq_ref, more_ref, up_ref, down_ref, o_ref):
    square = sq_ref[...] + more_ref[...]
    o_ref[...] = square + get_square(up_ref)[0:8] + get_square(down_ref)[0:8]


def square_sum(parts, after):
    return kernel_call(
        square_kernel,
        array(8, 128, dtype=F32),
        parts,
        [WHOLE] * 4,
        WHOLE,
        "square_sum",
        cost(0, 1 << 16),
        after=after,
    )


def row_sum(kernel, name, *parts, after=(), flops=0):
    return kernel_call(
        kernel,
        array(ROWS, D),
        parts,
        [WHOLE] * len(parts),
        WHOLE,
        name,
        cost(flops, ROWS * D * 2 * (len(parts) + 1)),
        after=after,
    )


def relay_kernel(
    own_low, own_high, mate_low, mate_high, term_up, term_down, up_ref, down_ref
):
    for n, (low, high) in enumerate(((own_low, own_high), (mate_low, mate_high))):
        part = slice(n * HALF_ROWS, (n + 1) * HALF_ROWS)
        up_ref[part, :] = low[0:HALF_ROWS, :]
        down_ref[part, :] = high[HALF_ROWS:ROWS, :]
    up_ref[ROWS : 2 * ROWS, :] = term_up[...]
    down_ref[ROWS : 2 * ROWS, :] = term_down[...]


def relay(parts, after):
    return kernel_call(
        relay_kernel,
        [array(2 * ROWS, D)] * 2,
        parts,
        [WHOLE] * 6,
        [WHOLE] * 2,
        "relay",
        cost(0, 4 << 20),
        after=after,
    )


def add_kernel(a_ref, b_ref, o_ref):
    o_ref[...] = a_ref[...] + b_ref[...]


def add_small(a, b, after):
    return kernel_call(
        add_kernel,
        array(8, 128, dtype=F32),
        (a, b),
        [WHOLE] * 2,
        WHOLE,
        "add_small",
        cost(0, 1 << 14),
        after=after,
    )


def grads_kernel(pos, *refs):
    pieces, (w_ref, t_ref, proj_ref, ctx_ref, sq_ref, held) = refs[:8], refs[8:]

    def place(dy, dl, piece, first=0):
        row = pl.multiple_of(token_block(pos, dy, dl) * ROWS + first, HALF_ROWS)
        held[pl.ds(row, piece.shape[0]), :] = piece

    for n, (dy, dl) in enumerate(((0, 0), (0, 1), (-1, 0), (-1, 1), (1, 0), (1, 1))):
        place(dy, dl, pieces[n][...])
    for dl in range(NL):
        part = slice(dl * HALF_ROWS, (dl + 1) * HALF_ROWS)
        place(2, dl, pieces[6][part, :])
        place(2, dl, pieces[7][part, :], HALF_ROWS)

    ctx_ref[...] = dot(held[...], w_ref[...], 1, 1).astype(BF)
    turned = t_ref[...]
    square = jnp.zeros((8, TILE), F32)
    for i in range(D // TILE):
        at = slice(i * TILE, (i + 1) * TILE)
        proj = dot(turned, held[:, at], 1, 0)
        proj_ref[:, at] = proj.astype(BF)
        square += jnp.sum((proj * proj).reshape(TOK // 8, 8, TILE), axis=0)
    sq_ref[...] = jnp.broadcast_to(jnp.sum(square, axis=(0, 1), keepdims=True), (8, 128))


def grads(pos, pieces, weight, turned, after):
    hq = GROUP * HD
    return kernel_call(
        grads_kernel,
        [array(hq, D), array(TOK, hq), array(8, 128, dtype=F32)],
        (*pieces, weight, turned),
        [WHOLE] * 10,
        [WHOLE] * 3,
        "grads",
        cost(4.3e9, 13 << 20),
        grid=(1,),
        pos=pos,
        scratch=[pltpu.VMEM((TOK, D), BF)],
        after=after,
    )


BLOCK = D // NX


def block_columns(pos, k, j, c):
    here = pl.multiple_of(share_column(pos, -k, -j, c) * SHARE, SHARE)
    local = pl.multiple_of((((pos[1] - j) % NZ) * 2 + (pos[2] + c) % 2) * SHARE, SHARE)
    return pl.ds(here, SHARE), pl.ds(local, SHARE)


def block_of(pos, k):
    return pl.ds(pl.multiple_of(((pos[0] - k) % NX) * BLOCK, BLOCK), BLOCK)


def mix_kernel(
    pos, sq_ref, more_ref, w_ref, p_ref, own, low, high, own_b, low_b, high_b, o_hbm, far_ref, held, sems
):
    square = sq_ref[0:1, 0:1] + more_ref[0:1, 0:1]
    rate = step_size / jnp.sqrt(square / (HEADS * HD * D) + eps_norm)
    rows = 64
    copies = []
    for n, (k, piece, other) in enumerate(
        ((0, own, own_b), (1, low, low_b), (3, high, high_b), (2, None, None))
    ):

        def step(i, carry, n=n, k=k, piece=piece, other=other):
            start = pl.multiple_of(i * rows, rows)
            here = pl.ds(start, rows)
            for c in range(2):
                for j in range(NZ):
                    at, local = block_columns(pos, k, j, c)
                    weight = w_ref[here, at].astype(F32)
                    stepped = (weight - rate * p_ref[here, at].astype(F32)).astype(BF)
                    value = (mix_share * stepped.astype(F32)).astype(BF)
                    wide = slice(j * SHARE, (j + 1) * SHARE)
                    if piece is None:
                        far_ref[here, local] = value
                    elif c == 0:
                        held[n, here, local] = value + piece[here, wide]
                    else:
                        held[n, here, local] = value + other[here, wide]
            return carry

        lax.fori_loop(0, TOK // rows, step, 0)
        if piece is not None:
            copies.append(
                pltpu.make_async_copy(held.at[n], o_hbm.at[:, block_of(pos, k)], sems.at[n])
            )
            copies[-1].start()
    for copy in copies:
        copy.wait()


def mix(pos, parts, after):
    return kernel_call(
        mix_kernel,
        [array(TOK, D), array(TOK, BLOCK)],
        parts,
        [WHOLE] * 10,
        [pl.BlockSpec(memory_space=pltpu.HBM), WHOLE],
        "mix",
        cost(0, 48 << 20),
        grid=(1,),
        pos=pos,
        scratch=[pltpu.VMEM((3, TOK, BLOCK), BF), pltpu.SemaphoreType.DMA((3,))],
        after=after,
    )


def mix_far_kernel(pos, f_ref, low, high, low_b, high_b, i_hbm, o_hbm, done_ref, held, sem):
    done_ref[...] = jnp.zeros_like(done_ref)
    for rows, pieces in ((FIRST, (low, low_b)), (LAST, (high, high_b))):
        for c, piece in enumerate(pieces):
            for j in range(NZ):
                _, local = block_columns(pos, 2, j, c)
                held[rows, local] = f_ref[rows, local] + piece[:, j * SHARE : (j + 1) * SHARE]
    copy = pltpu.make_async_copy(held, o_hbm.at[:, block_of(pos, 2)], sem)
    copy.start()
    copy.wait()


def mix_far(pos, parts, result):
    return kernel_call(
        mix_far_kernel,
        [array(TOK, D), array(8, 128, dtype=F32)],
        (*parts, result),
        [WHOLE] * 5 + [pl.BlockSpec(memory_space=pltpu.HBM)],
        [pl.BlockSpec(memory_space=pltpu.HBM), WHOLE],
        "mix_far",
        cost(0, 0),
        grid=(1,),
        pos=pos,
        scratch=[pltpu.VMEM((TOK, BLOCK), BF), pltpu.SemaphoreType.DMA],
        alias={6: 0},
    )


def per_device(queries, keys, values_in, out_grad, proj_local, outer_weight, momentum):
    r = lax.axis_index("replica")
    t = lax.axis_index("tensor")
    pos = jnp.stack([r // (NZ * 2), (r // 2) % NZ, r % 2, t // NL, t % NL]).astype(jnp.int32)

    def x_shift(v, d):
        return replica_shift(v, d % NX, 0, 0)

    def z_shift(v, d):
        return replica_shift(v, 0, d % NZ, 0)

    def y_shift(v, d):
        return tensor_shift(v, d % NY, 0)

    def mate_shift(v):
        return tensor_shift(v, 0, 1)

    def core_swap(v):
        return replica_shift(v, 0, 0, 1)

    weight, grad_own = proj_local[0], out_grad
    from_core = core_swap(open_step(pos, weight))
    grad_mate = mate_shift(grad_own)
    own_low, own_high = y_shift(grad_own, 1), y_shift(grad_own, -1)

    x_own, x_up, x_down, x_keep = core_add(pos, weight, from_core, ())
    x_low, x_high = x_shift(x_up, 1), x_shift(x_down, -1)
    context, turned = forward(queries, keys, values_in, (x_up,))
    grad_mate = hold(grad_mate, (context,))
    mate_low, mate_high = y_shift(grad_mate, 1), y_shift(grad_mate, -1)
    send_up, send_down, keep_up, keep_down, kept_own, kept_mate = term(
        pos, context, weight, (grad_mate,)
    )

    x_up2, x_down2 = ring_mid(x_keep, x_low, x_high, (kept_own, own_low, own_high))
    x_low2, x_high2 = x_shift(x_up2, 1), x_shift(x_down2, -1)
    z_own, *to_z = x_add((x_own, x_low, x_high, x_low2, x_high2))
    relay_up, relay_down = relay(
        (own_low, own_high, mate_low, mate_high, send_up, send_down), (z_own,)
    )
    relay_low, relay_high = y_shift(relay_up, 1), y_shift(relay_down, -1)
    from_z = [z_shift(to_z[j - 1], j) for j in (2, 1, 3)]
    new_outer, new_momentum, half = outer_update(
        (z_own, *from_z), outer_weight, momentum, ()
    )

    by_z = {j: z_shift(half, j) for j in (2, 1, 3)}
    pieces = (
        grad_own, grad_mate, own_low, mate_low, own_high, mate_high, relay_low, relay_high
    )
    proj_grad, ctx_grad, square = grads(pos, pieces, weight, turned, (half,))
    more = tensor_shift(square, 2, 0)
    send_up2, send_down2 = term_mid((keep_up, keep_down, relay_low, relay_high, square), (square,))
    term_low2, term_high2 = y_shift(send_up2, 1), y_shift(send_down2, -1)
    group = join_z((half, by_z[1], by_z[2], by_z[3]), (send_up2,))
    g_low, g_high = x_shift(group, 1), x_shift(group, -1)
    query_grad, key_grad, value_grad, done = backward(
        queries, keys, values_in, ctx_grad, (group,)
    )
    g_up2, g_down2 = cut(g_low, g_high, (done,))
    g_low2, g_high2 = x_shift(g_up2, 1), x_shift(g_down2, -1)
    square = square_sum((square, more, term_low2, term_high2), (g_up2,))
    more = mate_shift(square)
    send_mate = row_sum(mate_kernel, "mate_sum", kept_mate, term_low2, term_high2, after=(more,))
    term_mate = mate_shift(send_mate)
    near, late = (group, g_low, g_high), hold(group, (g_up2,))
    new_local, far = mix(
        pos,
        (square, more, weight, proj_grad, *near, *[core_swap(p) for p in (late, g_low, g_high)]),
        (send_mate,),
    )
    new_local, done = mix_far(
        pos, (far, g_low2, g_high2, core_swap(g_low2), core_swap(g_high2)), new_local
    )
    attn_out = row_sum(
        sum_kernel, "attn_sum", kept_own, term_low2, term_high2, term_mate, after=(done,)
    )
    return (attn_out, query_grad, key_grad, value_grad, new_local[None], new_outer, new_momentum)


def solution(mesh):
    return jax.shard_map(
        per_device,
        mesh=mesh,
        in_specs=(
            P("replica", "tensor"),
            P("replica", "tensor"),
            P("replica", "tensor"),
            P(("replica", "tensor"), None),
            P("replica", "tensor", None),
            P("tensor", "replica"),
            P("tensor", "replica"),
        ),
        out_specs=(
            P(("replica", "tensor"), None),
            P("replica", "tensor"),
            P("replica", "tensor"),
            P("replica", "tensor"),
            P("replica", "tensor", None),
            P("tensor", "replica"),
            P("tensor", "replica"),
        ),
        check_vma=False,
    )
```
